512 devices in a mesh: tm: 64 (over z, y_hi, core), space: 8 (over y_lo, x).
Axes of the slice: x: 4, y: 8 (y_hi: 4, y_lo: 2; y = y_hi * 2 + y_lo), z: 8, core: 2. Of those that a mesh axis runs over, the one named last changes fastest.
Arguments:
- fine_nodes: float32 [64, 3, 3, 64, 16, 128], P('tm', None, None, 'space'), may hold values from -4 to 4
- regions: int32 [64, 16, 128], P('space'), may hold values from 0 to 2
- activity: float32 [64, 16, 128], P('space'), may hold values from 0.3 to 3
- dirichlet: int32 [64, 16, 128], P('space'), may hold values 0 or 1
Outputs:
- next_nodes: float32 [64, 3, 3, 64, 16, 128], P('tm', None, None, 'space')
The draws below stay inside these ranges and needn't reach their ends.
All inputs are finite; a program needn't handle non-finite values. No bound on the sum of `dirichlet` on one device may be relied on, other than what follows from the above.
Results may differ from the reference program's by a relative error of at most 0.0003.
Values sent between devices are 32-bit elements; how exact they have to be, the bound alone decides.
No kernel may reach another device: no remote copies, remote signals or barrier semaphores. Data moves between devices by JAX's collectives and lax.ppermute only.
A program may use at most 64 MiB of HBM per device.

```python
import math
import jax
import jax.numpy as jnp
from jax import lax

NY = 16
NZ = 128
NODES = 3
FIELDS = 3
SLICES = 64
NX = 64


def plant(drawn, stream_key, smallest, high):
    index_at = [jax.random.randint(jax.random.fold_in(stream_key, axis), (), 0, length) for axis, length in enumerate(drawn.shape)]
    longest = drawn.shape.index(max(drawn.shape))
    neighbour = index_at[:longest] + [(index_at[longest] + 1) % drawn.shape[longest]] + index_at[longest + 1:]
    return drawn.at[tuple(index_at)].set(smallest).at[tuple(neighbour)].set(high)


def levels(rng, extent, pieces, least, largest):
    def one(axis_at, parts):
        steps = jax.random.uniform(jax.random.fold_in(jax.random.fold_in(rng, 6), axis_at), (parts,), jnp.float32, least / len(pieces), largest / len(pieces))
        return jnp.repeat(jnp.exp(steps), extent[axis_at] // parts).reshape((-1,) + (1,) * (len(extent) - axis_at - 1))

    factor_of = one(*pieces[0])
    for cut in pieces[1:]:
        factor_of = factor_of * one(*cut)
    return factor_of


def centred(key, shape, spread, bound, cuts=(), kind=jnp.bfloat16):
    result = jax.random.normal(key, shape, jnp.float32) * spread
    if len(cuts) > 0:
        result = levels(key, shape, cuts, -0.22, 0.18) * result
    return jnp.clip(result, min=-bound, max=bound).astype(kind)


def setup_inputs(seed: int = 0) -> dict:
    streams_of = jax.random.split(jax.random.key(seed), 5)
    fine_nodes = centred(streams_of[0], (SLICES, NODES, FIELDS, NX, NY, NZ), 0.6, 4.0, ((0, 64), (3, 8)), jnp.float32)
    regions = plant(jax.random.randint(streams_of[1], (NX, NY, NZ), 0, 3), jax.random.fold_in(streams_of[1], 1), 0, 2).astype(jnp.int32)
    activity = jnp.clip(jnp.exp(math.log(3.0) - 2.3025851 * jax.random.uniform(streams_of[2], (NX, NY, NZ), jnp.float32) ** levels(streams_of[2], (NX, NY, NZ), ((0, 8),), -0.2, 0.2)), 0.3, 3.0)
    dirichlet = plant((jax.random.randint(streams_of[3], (NX, NY, NZ), 0, 8) < 1).astype(jnp.int32), jax.random.fold_in(streams_of[3], 1), 0, 1)
    return dict(fine_nodes=fine_nodes, regions=regions, activity=activity, dirichlet=dirichlet)


time_step = 0.05
KAPPA_TABLE = ((1.0, 0.6, 1.4), (0.8, 1.2, 0.5), (0.7, 0.9, 1.1))
RELAX_RATES = (0.5, 1.0, 0.3)
SOURCE_SIGNS = (-1.0, -0.5, 0.25)


def cell_tables(regions, activity, dirichlet):
    kappa_table = jnp.asarray(KAPPA_TABLE, dtype=jnp.float32)
    conduct = jnp.zeros((3,) + regions.shape, jnp.float32)
    for r in range(3):
        in_region = (regions == r).astype(jnp.float32)
        conduct = conduct + kappa_table[:, r][:, None, None, None] * in_region[None]
    film_act = (regions == 0).astype(jnp.float32) * activity
    mobile = 1.0 - dirichlet.astype(jnp.float32)
    return conduct, film_act, mobile


def reaction(u, film_act):
    oxygen = u[..., 0, :, :, :]
    overpot = u[..., 1, :, :, :] - 0.5 * u[..., 2, :, :, :]
    forward = jnp.exp(0.5 * overpot)
    backward = jnp.exp(-0.5 * overpot)
    current = film_act * oxygen * (forward - backward)
    return current, forward, backward, oxygen


def sources(u, film_act):
    current = reaction(u, film_act)[0]
    return jnp.stack([SOURCE_SIGNS[k] * current for k in range(3)], axis=-4)


def explicit(u, padded, conduct, film_act, mobile):
    along_x = padded[..., 2:, :, :] + padded[..., :-2, :, :]
    widths_y = [(0, 0)] * (u.ndim - 2) + [(1, 1), (0, 0)]
    pad_y = jnp.pad(u, widths_y)
    along_y = pad_y[..., 2:, :] + pad_y[..., :-2, :]
    widths_z = [(0, 0)] * (u.ndim - 1) + [(1, 1)]
    pad_z = jnp.pad(u, widths_z)
    along_z = pad_z[..., 2:] + pad_z[..., :-2]
    laplace = along_x + along_y + along_z - 6.0 * u
    return mobile * (conduct * laplace + sources(u, film_act))


def restrict(v):
    shape = v.shape
    blocks = v.reshape(shape[:-3] + (shape[-3] // 2, 2, shape[-2] // 2, 2, shape[-1]))
    return 0.25 * jnp.sum(blocks, axis=(-4, -2))


def prolong(v):
    return jnp.repeat(jnp.repeat(v, 2, axis=-3), 2, axis=-2)


def matvec(matrix, v):
    return jnp.sum(matrix * v[None], axis=1)


def matmul(left, right):
    return jnp.sum(left[:, :, None] * right[None], axis=1)


def slice_work(node_vals, old_padded, padder, conduct, film_act, mobile):
    rates = jnp.asarray(RELAX_RATES, dtype=jnp.float32)[:, None, None, None]
    relax = rates * mobile[None]
    half_step = 0.5 * time_step
    old_expl = explicit(node_vals, old_padded, conduct, film_act, mobile)
    old_force = old_expl - relax * node_vals
    new_zero = node_vals[0]
    quad_one = time_step * (5.0 / 24.0 * old_force[0] + 1.0 / 3.0 * old_force[1] - 1.0 / 24.0 * old_force[2])
    new_one = (new_zero + half_step * relax * node_vals[1] + quad_one) / (1.0 + half_step * relax)
    expl_one = explicit(new_one, padder(new_one), conduct, film_act, mobile)
    quad_two = time_step * (-1.0 / 24.0 * old_force[0] + 1.0 / 3.0 * old_force[1] + 5.0 / 24.0 * old_force[2])
    new_two = (new_one + half_step * (expl_one - old_expl[1]) + half_step * relax * node_vals[2] + quad_two) / (1.0 + half_step * relax)
    expl_two = explicit(new_two, padder(new_two), conduct, film_act, mobile)
    force_one = expl_one - relax * new_one
    force_two = expl_two - relax * new_two
    integral = time_step * (old_force[0] / 6.0 + 2.0 / 3.0 * force_one + force_two / 6.0)
    coarse_zero = restrict(new_zero)
    coarse_one = restrict(new_two)
    cfilm = restrict(film_act)
    cmobile = restrict(mobile)
    crelax = rates * cmobile[None]
    tend_zero = cmobile * sources(coarse_zero, cfilm) - crelax * coarse_zero
    tend_one = cmobile * sources(coarse_one, cfilm) - crelax * coarse_one
    fas_term = restrict(integral) - 0.5 * time_step * (tend_zero + tend_one)
    current, forward, backward, oxygen = reaction(coarse_zero, cfilm)
    derivs = jnp.stack([cfilm * (forward - backward), cfilm * oxygen * 0.5 * (forward + backward), cfilm * oxygen * (-0.25) * (forward + backward)], axis=0)
    jacobian = jnp.stack([SOURCE_SIGNS[k] * derivs for k in range(3)], axis=0)
    divisor = 1.0 + time_step * crelax
    identity = jnp.eye(3, dtype=jnp.float32)[:, :, None, None, None]
    matrix = (identity + time_step * cmobile * jacobian) / divisor[:, None]
    jac_start = matvec(jacobian, coarse_zero)
    offset = (-time_step * cmobile * jac_start + time_step * crelax * coarse_one + 0.5 * time_step * (tend_zero + tend_one) + fas_term) / divisor
    return jnp.stack([new_zero, new_one, new_two]), coarse_zero, coarse_one, matrix, offset


def correct(new_vals, coarse_start, coarse_end, coarse_zero, coarse_one):
    delta_zero = coarse_start - coarse_zero
    delta_one = coarse_end - coarse_one
    return jnp.stack([new_vals[0] + prolong(delta_zero), new_vals[1] + prolong(0.5 * (delta_zero + delta_one)), new_vals[2] + prolong(delta_one)])


def pad_single(u):
    return jnp.pad(u, ((0, 0), (1, 1), (0, 0), (0, 0)))


def reference(fine_nodes, regions, activity, dirichlet):
    conduct, film_act, mobile = cell_tables(regions, activity, dirichlet)

    def per_slice(node_vals):
        padded = jnp.pad(node_vals, ((0, 0), (0, 0), (1, 1), (0, 0), (0, 0)))
        return slice_work(node_vals, padded, pad_single, conduct, film_act, mobile)

    new_vals, zeros_c, ones_c, matrices, offsets = lax.map(per_slice, fine_nodes)

    def advance(v, item):
        return matvec(item[0], v) + item[1], v

    unused, start_values = lax.scan(advance, zeros_c[0], (matrices, offsets))

    def finish(item):
        coarse_end = matvec(item[1], item[2]) + item[3]
        return correct(item[0], item[2], coarse_end, item[4], item[5])

    corrected = lax.map(finish, (new_vals, matrices, start_values, offsets, zeros_c, ones_c))
    head_nodes = jnp.concatenate([corrected[:1, 0], corrected[:-1, 2]], axis=0)
    return corrected.at[:, 0].set(head_nodes)
```

```python
import jax
import jax.numpy as jnp
from jax import lax
from jax.experimental import pallas as pl
from jax.experimental.pallas import tpu as pltpu
from jax.sharding import PartitionSpec as P

DT = 0.05
H = 0.5 * DT
KAPPA = ((1.0, 0.6, 1.4), (0.8, 1.2, 0.5), (0.7, 0.9, 1.1))
RATES = (0.5, 1.0, 0.3)
SIGNS = (-1.0, -0.5, 0.25)
Q1 = (DT * 5.0 / 24.0, DT / 3.0, -DT / 24.0)
Q2 = (-DT / 24.0, DT / 3.0, DT * 5.0 / 24.0)
Q3 = (DT / 6.0, DT * 2.0 / 3.0, DT / 6.0)
ROWS = 16
LANES = 128
EDGE = 18


def combine(weights, states):
    total = weights[0] * states[0]
    for w, s in zip(weights[1:], states[1:]):
        total = total + w * s
    return total


def shifted(v):
    rows = v.shape[0]
    y = lax.rem(lax.broadcasted_iota(jnp.int32, v.shape, 0), ROWS)
    z = lax.broadcasted_iota(jnp.int32, v.shape, 1)
    up = jnp.where(y == 0, 0.0, pltpu.roll(v, 1, 0))
    down = jnp.where(y == ROWS - 1, 0.0, pltpu.roll(v, rows - 1, 0))
    left = jnp.where(z == 0, 0.0, pltpu.roll(v, 1, 1))
    right = jnp.where(z == LANES - 1, 0.0, pltpu.roll(v, LANES - 1, 1))
    return (up + down) + (left + right)


def laplace(v):
    mid = v[ROWS:-ROWS]
    return v[: -2 * ROWS] + v[2 * ROWS :] + shifted(mid) - 6.0 * mid


def reaction(o, p, q):
    over = 0.5 * (p - 0.5 * q)
    return jnp.exp(over), jnp.exp(-over)


def current(state, film):
    fwd, bwd = reaction(*state)
    return film * state[0] * (fwd - bwd)


def conduct(region, k):
    return jnp.where(region == 0.0, KAPPA[k][0], jnp.where(region == 1.0, KAPPA[k][1], KAPPA[k][2]))


def inverse(mobile, k):
    return 1.0 - mobile * (H * RATES[k] / (1.0 + H * RATES[k]))


def first_new(old, lap, region, film, mobile):
    flow = combine(Q1, [current(old[m], film) for m in range(3)])
    news = []
    for k in range(3):
        w1 = combine(Q1, [old[m][k] for m in range(3)])
        inner = conduct(region, k) * lap[k] + SIGNS[k] * flow + RATES[k] * (H * old[1][k] - w1)
        news.append((old[0][k] + mobile * inner) * inverse(mobile, k))
    return news


def w2_of(old, k):
    return combine((Q2[0], Q2[1] - H, Q2[2]), [old[m][k] for m in range(3)])


def planes(lo, hi):
    return pl.ds(lo * ROWS, (hi - lo) * ROWS)


def edge_kernel(u, regions, activity, dirichlet, low_out, high_out):
    def tables(at):
        region = regions[at].astype(jnp.float32)
        film = jnp.where(region == 0.0, activity[at], 0.0)
        return region, film, 1.0 - dirichlet[at].astype(jnp.float32)

    for out, edge, inner, three in ((low_out, 0, 1, 0), (high_out, 7, 6, 5)):
        at = planes(inner, inner + 1)
        old = [[u[m * 3 + k, at] for k in range(3)] for m in range(3)]
        wide = planes(three, three + 3)
        lap = []
        for k in range(3):
            w1 = combine(Q1, [u[m * 3 + k, wide] for m in range(3)])
            out[9 + k] = w1[ROWS : 2 * ROWS]
            lap.append(laplace(w1))
        news = first_new(old, lap, *tables(at))
        for k in range(3):
            out[12 + k] = H * news[k] + w2_of(old, k)
        end = planes(edge, edge + 1)
        for i in range(9):
            out[i] = u[i, end]
        for i, table in enumerate(tables(end)):
            out[15 + i] = table


def main_kernel(u, regions, activity, dirichlet, low, high, new1_out, new2_out, payload, local, scratch):
    def wrap(inside, i):
        return jnp.concatenate([low[i], inside, high[i]], axis=0)

    region = wrap(regions[...].astype(jnp.float32), 15)
    film = wrap(jnp.where(regions[...] == 0, activity[...], 0.0), 16)
    mobile = wrap(1.0 - dirichlet[...].astype(jnp.float32), 17)
    old = [[wrap(u[m * 3 + k], m * 3 + k) for k in range(3)] for m in range(3)]
    lap1 = []
    for k in range(3):
        w1 = combine(Q1, [old[m][k] for m in range(3)])
        lap1.append(laplace(jnp.concatenate([low[9 + k], w1, high[9 + k]], axis=0)))
    new1 = first_new(old, lap1, region, film, mobile)
    flows = [current(old[m], film) for m in range(3)]
    flow2 = combine((Q2[0], Q2[1] - H, Q2[2]), flows) + H * current(new1, film)
    new2 = []
    for k in range(3):
        v2 = H * new1[k] + w2_of(old, k)
        lap2 = laplace(jnp.concatenate([low[12 + k], v2, high[12 + k]], axis=0))
        decay = H * old[2][k] - combine(Q2, [old[m][k] for m in range(3)])
        inner = conduct(region, k) * lap2 + SIGNS[k] * flow2 + RATES[k] * decay
        new2.append((new1[k] + mobile * inner) * inverse(mobile, k))
    mid = slice(ROWS, -ROWS)
    flow3 = combine(Q3, [flows[0][mid], current([v[mid] for v in new1], film[mid]), current([v[mid] for v in new2], film[mid])])

    def restrict(i, v):
        pairs = v.reshape(4, 2, ROWS, LANES)
        scratch[i] = (pairs[:, 0] + pairs[:, 1]).reshape(4 * ROWS, LANES)
        return 0.25 * (scratch[i, pl.ds(0, 32, stride=2)] + scratch[i, pl.ds(1, 32, stride=2)])

    region, mobile_mid, film_mid = region[mid], mobile[mid], film[mid]
    integral, zero, one = [], [], []
    for k in range(3):
        v3 = combine(Q3, [old[0][k], new1[k], new2[k]])
        force = mobile_mid * (conduct(region, k) * laplace(v3) + SIGNS[k] * flow3 - RATES[k] * v3[mid])
        integral.append(restrict(k, force))
        new1_out[k] = new1[k][mid]
        new2_out[k] = new2[k][mid]
        zero.append(restrict(3 + k, old[0][k][mid]))
        one.append(restrict(6 + k, new2[k][mid]))
    cfilm = restrict(9, film_mid)
    cmobile = restrict(10, mobile_mid)
    fwd, bwd = reaction(*zero)
    scale = (DT * cmobile) * cfilm
    a = scale * (fwd - bwd)
    b = scale * zero[0] * 0.5 * (fwd + bwd)
    slope = a * zero[0] + b * (zero[1] - 0.5 * zero[2])
    flow_c = (cfilm * zero[0] * (fwd - bwd)) + current(one, cfilm)
    is_first = lax.axis_index("tm") == 0
    local[3] = a
    local[4] = b
    local[5] = cmobile
    sent = []
    for k in range(3):
        tend = H * cmobile * (SIGNS[k] * flow_c - RATES[k] * (zero[k] + one[k]))
        fas = integral[k] - tend
        term = (DT * RATES[k]) * cmobile * one[k] - SIGNS[k] * slope + tend + fas
        local[k] = term
        local[6 + k] = zero[k]
        local[9 + k] = one[k]
        sent.append(jnp.where(is_first, term + zero[k] + SIGNS[k] * slope, term))
    sent += [jnp.where(is_first, 0.0, a), jnp.where(is_first, 0.0, b), jnp.zeros_like(a)]
    lane = lax.broadcasted_iota(jnp.int32, (32, LANES), 1)
    half = lane < 64
    for m in range(3):
        x, y = sent[2 * m], sent[2 * m + 1]
        payload[pl.ds(m, 32, stride=8)] = jnp.where(half, x, pltpu.roll(y, 64, 1))
        payload[pl.ds(4 + m, 32, stride=8)] = jnp.where(half, pltpu.roll(x, 64, 1), y)
    payload[pl.ds(3, 32, stride=8)] = jnp.zeros_like(a)
    payload[pl.ds(7, 32, stride=8)] = jnp.zeros_like(a)


def scan_kernel(arrived, local, out, rolled, states):
    me = lax.axis_index("tm")
    row = local[5, pl.ds(me // 2, 1)]
    cmobile = jnp.where(lax.rem(me, 2) == 0, row, pltpu.roll(row, 64, 1))
    keep = [1.0 / (1.0 + (DT * RATES[k]) * cmobile) for k in range(3)]
    rolled[...] = pltpu.roll(arrived[...], 64, 1)
    v = [jnp.zeros((1, LANES), jnp.float32) for _ in range(3)]
    for n in range(64):
        for k in range(3):
            states[k, pl.ds(n, 1)] = v[k]
        term = [arrived[pl.ds(4 * n, 1)], rolled[pl.ds(4 * n, 1)], arrived[pl.ds(4 * n + 1, 1)]]
        a, b = rolled[pl.ds(4 * n + 1, 1)], arrived[pl.ds(4 * n + 2, 1)]
        t = a * v[0] + b * (v[1] - 0.5 * v[2])
        v = [keep[k] * (v[k] + term[k] + SIGNS[k] * t) for k in range(3)]
    half = lax.broadcasted_iota(jnp.int32, (64, LANES), 1) < 64
    out[pl.ds(0, 64, stride=2)] = jnp.where(half, states[0], pltpu.roll(states[1], 64, 1))
    out[pl.ds(1, 64, stride=2)] = states[2]


def finish_kernel(u, new1, new2, behind, local, starts, out, scratch):
    is_first = lax.axis_index("tm") == 0
    half = lax.broadcasted_iota(jnp.int32, (32, LANES), 1) < 64
    rows = [starts[pl.ds(i, 32, stride=4)] for i in range(4)]
    start = [
        jnp.where(half, rows[0], pltpu.roll(rows[2], 64, 1)),
        jnp.where(half, pltpu.roll(rows[0], 64, 1), rows[2]),
        jnp.where(half, rows[1], pltpu.roll(rows[3], 64, 1)),
    ]
    start = [jnp.where(is_first, local[6 + k], start[k]) for k in range(3)]
    t = local[3] * start[0] + local[4] * (start[1] - 0.5 * start[2])

    def prolong(i, v):
        scratch[i, pl.ds(0, 32, stride=2)] = v
        scratch[i, pl.ds(1, 32, stride=2)] = v
        wide = scratch[i].reshape(4, 1, ROWS, LANES)
        return jnp.broadcast_to(wide, (4, 2, ROWS, LANES)).reshape(8 * ROWS, LANES)

    for k in range(3):
        end = (start[k] + local[k] + SIGNS[k] * t) / (1.0 + (DT * RATES[k]) * local[5])
        delta_zero = start[k] - local[6 + k]
        delta_one = end - local[9 + k]
        head = jnp.where(is_first, u[k], behind[k])
        pairs = head.reshape(4, 2, ROWS, LANES)
        scratch[9 + k] = (pairs[:, 0] + pairs[:, 1]).reshape(4 * ROWS, LANES)
        coarse = 0.25 * (scratch[9 + k, pl.ds(0, 32, stride=2)] + scratch[9 + k, pl.ds(1, 32, stride=2)])
        out[k] = head + prolong(3 * k, start[k] - coarse)
        out[3 + k] = new1[k] + prolong(3 * k + 1, 0.5 * (delta_zero + delta_one))
        out[6 + k] = new2[k] + prolong(3 * k + 2, delta_one)


def call(kernel, outs, scratch, *args):
    return pl.pallas_call(
        kernel,
        out_shape=[jax.ShapeDtypeStruct(s, jnp.float32) for s in outs],
        in_specs=[pl.BlockSpec(memory_space=pltpu.VMEM)] * len(args),
        out_specs=[pl.BlockSpec(memory_space=pltpu.VMEM)] * len(outs),
        scratch_shapes=[pltpu.VMEM(s, jnp.float32) for s in scratch],
        compiler_params=pltpu.CompilerParams(vmem_limit_bytes=32 * 1024 * 1024),
    )(*args)


def on_device(fine_nodes, regions, activity, dirichlet):
    u = fine_nodes.reshape(9, 128, LANES)
    tables = [v.reshape(128, LANES) for v in (regions, activity, dirichlet)]
    edge = (EDGE, ROWS, LANES)
    to_low, to_high = call(edge_kernel, [edge, edge], [], u, *tables)
    count = lax.axis_size("space")
    low = lax.ppermute(to_high, "space", [(i, i + 1) for i in range(count - 1)])
    high = lax.ppermute(to_low, "space", [(i + 1, i) for i in range(count - 1)])
    brick = (3, 128, LANES)
    new1, new2, payload, local = call(
        main_kernel, [brick, brick, (256, LANES), (12, 32, LANES)], [(11, 64, LANES)], u, *tables, low, high
    )
    slices = lax.axis_size("tm")
    behind = lax.ppermute(new2, "tm", [(i, i + 1) for i in range(slices - 1)])
    arrived = lax.all_to_all(payload, "tm", 0, 0, tiled=True)
    (starts,) = call(scan_kernel, [(128, LANES)], [(256, LANES), (3, 64, LANES)], arrived, local)
    starts = lax.all_to_all(starts, "tm", 0, 0, tiled=True)
    (out,) = call(finish_kernel, [(9, 128, LANES)], [(12, 64, LANES)], u, new1, new2, behind, local, starts)
    return out.reshape(fine_nodes.shape)


def solution(mesh):
    whole = P("tm", None, None, "space", None, None)
    part = P("space", None, None)
    return jax.shard_map(
        on_device, mesh=mesh, in_specs=(whole, part, part, part), out_specs=whole, check_vma=False
    )
```

```python
import jax
import jax.numpy as jnp
from jax import lax
from jax.experimental import pallas as pl
from jax.experimental.pallas import tpu as pltpu
from jax.sharding import PartitionSpec as P

DT = 0.05
H = 0.5 * DT
KAPPA = ((1.0, 0.6, 1.4), (0.8, 1.2, 0.5), (0.7, 0.9, 1.1))
RATES = (0.5, 1.0, 0.3)
SIGNS = (-1.0, -0.5, 0.25)
Q1 = (DT * 5.0 / 24.0, DT / 3.0, -DT / 24.0)
Q2 = (-DT / 24.0, DT / 3.0, DT * 5.0 / 24.0)
Q3 = (DT / 6.0, DT * 2.0 / 3.0, DT / 6.0)
ROWS = 16
LANES = 128
EDGE = 18


def combine(weights, states):
    total = weights[0] * states[0]
    for w, s in zip(weights[1:], states[1:]):
        total = total + w * s
    return total


def shifted(v):
    rows = v.shape[0]
    y = lax.rem(lax.broadcasted_iota(jnp.int32, v.shape, 0), ROWS)
    z = lax.broadcasted_iota(jnp.int32, v.shape, 1)
    up = jnp.where(y == 0, 0.0, pltpu.roll(v, 1, 0))
    down = jnp.where(y == ROWS - 1, 0.0, pltpu.roll(v, rows - 1, 0))
    left = jnp.where(z == 0, 0.0, pltpu.roll(v, 1, 1))
    right = jnp.where(z == LANES - 1, 0.0, pltpu.roll(v, LANES - 1, 1))
    return (up + down) + (left + right)


def laplace(v):
    mid = v[ROWS:-ROWS]
    return v[: -2 * ROWS] + v[2 * ROWS :] + shifted(mid) - 6.0 * mid


def reaction(o, p, q):
    over = 0.5 * (p - 0.5 * q)
    return jnp.exp(over), jnp.exp(-over)


def current(state, film):
    fwd, bwd = reaction(*state)
    return film * state[0] * (fwd - bwd)


def conduct(region, k):
    return jnp.where(region == 0.0, KAPPA[k][0], jnp.where(region == 1.0, KAPPA[k][1], KAPPA[k][2]))


def inverse(mobile, k):
    return 1.0 - mobile * (H * RATES[k] / (1.0 + H * RATES[k]))


def first_new(old, lap, region, film, mobile):
    flow = combine(Q1, [current(old[m], film) for m in range(3)])
    news = []
    for k in range(3):
        w1 = combine(Q1, [old[m][k] for m in range(3)])
        inner = conduct(region, k) * lap[k] + SIGNS[k] * flow + RATES[k] * (H * old[1][k] - w1)
        news.append((old[0][k] + mobile * inner) * inverse(mobile, k))
    return news


def w2_of(old, k):
    return combine((Q2[0], Q2[1] - H, Q2[2]), [old[m][k] for m in range(3)])


def planes(lo, hi):
    return pl.ds(lo * ROWS, (hi - lo) * ROWS)


def copy_all(pairs, sems):
    copies = [pltpu.make_async_copy(src, dst, sems.at[i]) for i, (src, dst) in enumerate(pairs)]
    for copy in copies:
        copy.start()
    for copy in copies:
        copy.wait()


def edge_kernel(u_far, regions_far, activity_far, dirichlet_far, low_out, high_out, u, ints, activity, sems):
    pairs = []
    for side, three, two in ((0, 0, 0), (1, 5, 6)):
        wide, at = planes(three, three + 3), planes(two, two + 2)
        pairs.append((u_far.at[:, wide], u.at[side]))
        pairs.append((regions_far.at[at], ints.at[side, 0]))
        pairs.append((dirichlet_far.at[at], ints.at[side, 1]))
        pairs.append((activity_far.at[at], activity.at[side]))
    copy_all(pairs, sems)

    def tables(side, plane):
        at = planes(plane, plane + 1)
        region = ints[side, 0, at].astype(jnp.float32)
        film = jnp.where(region == 0.0, activity[side, at], 0.0)
        return region, film, 1.0 - ints[side, 1, at].astype(jnp.float32)

    mid = planes(1, 2)
    for side, out, edge in ((0, low_out, 0), (1, high_out, 2)):
        old = [[u[side, m * 3 + k, mid] for k in range(3)] for m in range(3)]
        lap = []
        for k in range(3):
            w1 = combine(Q1, [u[side, m * 3 + k] for m in range(3)])
            out[9 + k] = w1[ROWS : 2 * ROWS]
            lap.append(laplace(w1))
        news = first_new(old, lap, *tables(side, 1 - side))
        for k in range(3):
            out[12 + k] = H * news[k] + w2_of(old, k)
        end = planes(edge, edge + 1)
        for i in range(9):
            out[i] = u[side, i, end]
        for i, table in enumerate(tables(side, side)):
            out[15 + i] = table


def restrict(scratch, i, v):
    pairs = v.reshape(4, 2, ROWS, LANES)
    scratch[i] = (pairs[:, 0] + pairs[:, 1]).reshape(4 * ROWS, LANES)
    return 0.25 * (scratch[i, pl.ds(0, 32, stride=2)] + scratch[i, pl.ds(1, 32, stride=2)])


def inner_kernel(u, regions, activity, dirichlet, fine, coarse, scratch):
    region = regions[...].astype(jnp.float32)
    film = jnp.where(regions[...] == 0, activity[...], 0.0)
    mobile = 1.0 - dirichlet[...].astype(jnp.float32)
    old = [[u[m * 3 + k] for k in range(3)] for m in range(3)]
    zeros = jnp.zeros((ROWS, LANES), jnp.float32)
    lap1 = []
    for k in range(3):
        w1 = combine(Q1, [old[m][k] for m in range(3)])
        fine[9 + k] = w1
        lap1.append(laplace(jnp.concatenate([zeros, w1, zeros], axis=0)))
    new1 = first_new(old, lap1, region, film, mobile)
    flows = [current(old[m], film) for m in range(3)]
    flow2 = combine((Q2[0], Q2[1] - H, Q2[2]), flows)
    fine[12] = flows[0]
    for k in range(3):
        fine[k] = new1[k]
        fine[3 + k] = w2_of(old, k)
        decay = H * old[2][k] - combine(Q2, [old[m][k] for m in range(3)])
        fine[6 + k] = SIGNS[k] * flow2 + RATES[k] * decay
    zero = [restrict(scratch, k, old[0][k]) for k in range(3)]
    cfilm = restrict(scratch, 3, film)
    cmobile = restrict(scratch, 4, mobile)
    fwd, bwd = reaction(*zero)
    scale = (DT * cmobile) * cfilm
    coarse[0] = scale * (fwd - bwd)
    coarse[1] = scale * zero[0] * 0.5 * (fwd + bwd)
    coarse[2] = cmobile
    coarse[3] = cfilm
    coarse[4] = cfilm * zero[0] * (fwd - bwd)
    for k in range(3):
        coarse[5 + k] = zero[k]


def outer_new1(near, side):
    old = [[side[m * 3 + k] for k in range(3)] for m in range(3)]
    lap = []
    for k in range(3):
        w1 = combine(Q1, [old[m][k] for m in range(3)])
        lap.append(side[9 + k] + near[k] + shifted(w1) - 6.0 * w1)
    return first_new(old, lap, side[15], side[16], side[17])


def outer_rest(side):
    old = [[side[m * 3 + k] for k in range(3)] for m in range(3)]
    flow2 = combine((Q2[0], Q2[1] - H, Q2[2]), [current(old[m], side[16]) for m in range(3)])
    rest = []
    for k in range(3):
        decay = H * old[2][k] - combine(Q2, [old[m][k] for m in range(3)])
        rest.append(SIGNS[k] * flow2 + RATES[k] * decay)
    return rest, [w2_of(old, k) for k in range(3)]


def main_kernel(u, regions, activity, dirichlet, fine, coarse, low, high, new1_out, new2_out, payload, local, scratch):
    def wrap(first, inside, last):
        return jnp.concatenate([first, inside, last], axis=0)

    own_region = regions[...].astype(jnp.float32)
    own_mobile = 1.0 - dirichlet[...].astype(jnp.float32)
    own_film = jnp.where(regions[...] == 0, activity[...], 0.0)
    region = wrap(low[15], own_region, high[15])
    film = wrap(low[16], own_film, high[16])
    mobile = wrap(low[17], own_mobile, high[17])
    first, last, between = slice(0, ROWS), slice(7 * ROWS, 8 * ROWS), slice(ROWS, 7 * ROWS)
    below = outer_new1([fine[9 + k, planes(0, 1)] for k in range(3)], low)
    above = outer_new1([fine[9 + k, planes(7, 8)] for k in range(3)], high)
    low_rest, low_w2 = outer_rest(low)
    high_rest, high_w2 = outer_rest(high)
    new1, own1 = [], []
    for k in range(3):
        v = fine[k]
        ends = []
        for at, side in ((first, low), (last, high)):
            factor = own_mobile[at] * inverse(own_mobile[at], k) * conduct(own_region[at], k)
            ends.append(v[at] + factor * combine(Q1, [side[m * 3 + k] for m in range(3)]))
        v = jnp.concatenate([ends[0], v[between], ends[1]], axis=0)
        own1.append(v)
        new1_out[k] = v
        new1.append(wrap(below[k], v, above[k]))
    flow1 = H * current(new1, film)
    new2, own2 = [], []
    for k in range(3):
        w2 = wrap(low_w2[k], fine[3 + k], high_w2[k])
        v2 = H * new1[k] + w2
        lap2 = laplace(jnp.concatenate([low[12 + k], v2, high[12 + k]], axis=0))
        rest = wrap(low_rest[k], fine[6 + k], high_rest[k])
        inner = conduct(region, k) * lap2 + SIGNS[k] * flow1 + rest
        v = (new1[k] + mobile * inner) * inverse(mobile, k)
        new2.append(v)
        own2.append(v[ROWS:-ROWS])
        new2_out[k] = own2[k]
    flow3 = Q3[0] * fine[12] + (Q3[1] / H) * flow1[ROWS:-ROWS] + Q3[2] * current(own2, own_film)
    integral, one = [], []
    for k in range(3):
        ends = [combine(Q3, [side[k], new1[k][at], new2[k][at]]) for side, at in ((low, slice(0, ROWS)), (high, slice(9 * ROWS, 10 * ROWS)))]
        v3 = combine(Q3, [u[k], own1[k], own2[k]])
        lap3 = laplace(wrap(ends[0], v3, ends[1]))
        force = own_mobile * (conduct(own_region, k) * lap3 + SIGNS[k] * flow3 - RATES[k] * v3)
        integral.append(restrict(scratch, k, force))
        one.append(restrict(scratch, 3 + k, own2[k]))
    a, b, cmobile, cfilm = (coarse[i] for i in range(4))
    zero = [coarse[5 + k] for k in range(3)]
    slope = a * zero[0] + b * (zero[1] - 0.5 * zero[2])
    flow_c = coarse[4] + current(one, cfilm)
    is_first = lax.axis_index("tm") == 0
    local[3] = a
    local[4] = b
    local[5] = cmobile
    sent = []
    for k in range(3):
        tend = H * cmobile * (SIGNS[k] * flow_c - RATES[k] * (zero[k] + one[k]))
        fas = integral[k] - tend
        term = (DT * RATES[k]) * cmobile * one[k] - SIGNS[k] * slope + tend + fas
        local[k] = term
        local[6 + k] = zero[k]
        local[9 + k] = one[k]
        sent.append(jnp.where(is_first, term + zero[k] + SIGNS[k] * slope, term))
    sent += [jnp.where(is_first, 0.0, a), jnp.where(is_first, 0.0, b), jnp.zeros_like(a)]
    lane = lax.broadcasted_iota(jnp.int32, (32, LANES), 1)
    half = lane < 64
    for m in range(3):
        x, y = sent[2 * m], sent[2 * m + 1]
        payload[pl.ds(m, 32, stride=8)] = jnp.where(half, x, pltpu.roll(y, 64, 1))
        payload[pl.ds(4 + m, 32, stride=8)] = jnp.where(half, pltpu.roll(x, 64, 1), y)
    payload[pl.ds(3, 32, stride=8)] = jnp.zeros_like(a)
    payload[pl.ds(7, 32, stride=8)] = jnp.zeros_like(a)


def scan_kernel(arrived, local, out, rolled, states):
    me = lax.axis_index("tm")
    row = local[5, pl.ds(me // 2, 1)]
    cmobile = jnp.where(lax.rem(me, 2) == 0, row, pltpu.roll(row, 64, 1))
    keep = [1.0 / (1.0 + (DT * RATES[k]) * cmobile) for k in range(3)]
    rolled[...] = pltpu.roll(arrived[...], 64, 1)
    v = [jnp.zeros((1, LANES), jnp.float32) for _ in range(3)]
    for n in range(64):
        for k in range(3):
            states[k, pl.ds(n, 1)] = v[k]
        term = [arrived[pl.ds(4 * n, 1)], rolled[pl.ds(4 * n, 1)], arrived[pl.ds(4 * n + 1, 1)]]
        a, b = rolled[pl.ds(4 * n + 1, 1)], arrived[pl.ds(4 * n + 2, 1)]
        t = a * v[0] + b * (v[1] - 0.5 * v[2])
        v = [keep[k] * (v[k] + term[k] + SIGNS[k] * t) for k in range(3)]
    half = lax.broadcasted_iota(jnp.int32, (64, LANES), 1) < 64
    out[pl.ds(0, 64, stride=2)] = jnp.where(half, states[0], pltpu.roll(states[1], 64, 1))
    out[pl.ds(1, 64, stride=2)] = states[2]


def finish_kernel(u, new1, new2, behind, local, starts, far, out, scratch, sems):
    is_first = lax.axis_index("tm") == 0
    half = lax.broadcasted_iota(jnp.int32, (32, LANES), 1) < 64
    rows = [starts[pl.ds(i, 32, stride=4)] for i in range(4)]
    start = [
        jnp.where(half, rows[0], pltpu.roll(rows[2], 64, 1)),
        jnp.where(half, pltpu.roll(rows[0], 64, 1), rows[2]),
        jnp.where(half, rows[1], pltpu.roll(rows[3], 64, 1)),
    ]
    start = [jnp.where(is_first, local[6 + k], start[k]) for k in range(3)]
    t = local[3] * start[0] + local[4] * (start[1] - 0.5 * start[2])

    def prolong(i, v):
        scratch[i, pl.ds(0, 32, stride=2)] = v
        scratch[i, pl.ds(1, 32, stride=2)] = v
        wide = scratch[i].reshape(4, 1, ROWS, LANES)
        return jnp.broadcast_to(wide, (4, 2, ROWS, LANES)).reshape(8 * ROWS, LANES)

    copies = []
    for k in range(3):
        end = (start[k] + local[k] + SIGNS[k] * t) / (1.0 + (DT * RATES[k]) * local[5])
        delta_zero = start[k] - local[6 + k]
        delta_one = end - local[9 + k]
        head = jnp.where(is_first, u[k], behind[k])
        pairs = head.reshape(4, 2, ROWS, LANES)
        scratch[9 + k] = (pairs[:, 0] + pairs[:, 1]).reshape(4 * ROWS, LANES)
        coarse = 0.25 * (scratch[9 + k, pl.ds(0, 32, stride=2)] + scratch[9 + k, pl.ds(1, 32, stride=2)])
        parts = (
            head + prolong(3 * k, start[k] - coarse),
            new1[k] + prolong(3 * k + 1, 0.5 * (delta_zero + delta_one)),
            new2[k] + prolong(3 * k + 2, delta_one),
        )
        for m in range(3):
            out[3 * m + k] = parts[m]
            copy = pltpu.make_async_copy(out.at[3 * m + k], far.at[3 * m + k], sems.at[3 * m + k])
            copy.start()
            copies.append(copy)
    for copy in copies:
        copy.wait()


def call(kernel, outs, scratch, *args, near=True, near_out=True, cost=0, mib=32):
    vmem, hbm = pl.BlockSpec(memory_space=pltpu.VMEM), pl.BlockSpec(memory_space=pltpu.HBM)
    return pl.pallas_call(
        kernel,
        out_shape=[jax.ShapeDtypeStruct(s, jnp.float32) for s in outs],
        in_specs=[vmem if near else hbm] * len(args),
        out_specs=[vmem if near_out else hbm] * len(outs),
        scratch_shapes=scratch,
        compiler_params=pltpu.CompilerParams(vmem_limit_bytes=mib * 1024 * 1024),
        cost_estimate=pl.CostEstimate(flops=cost, bytes_accessed=cost, transcendentals=0),
    )(*args)


def f32(*shape):
    return pltpu.VMEM(shape, jnp.float32)


def on_device(fine_nodes, regions, activity, dirichlet):
    u = fine_nodes.reshape(9, 128, LANES)
    tables = [v.reshape(128, LANES) for v in (regions, activity, dirichlet)]
    edge = (EDGE, ROWS, LANES)
    buffers = [f32(2, 9, 48, LANES), pltpu.VMEM((2, 2, 32, LANES), jnp.int32), f32(2, 32, LANES), pltpu.SemaphoreType.DMA((8,))]
    pinned = [pltpu.with_memory_space_constraint(v, pltpu.HBM) for v in (u, *tables)]
    to_low, to_high = call(edge_kernel, [edge, edge], buffers, *pinned, near=False, cost=1000000, mib=32)
    count = lax.axis_size("space")
    low = lax.ppermute(to_high, "space", [(i, i + 1) for i in range(count - 1)])
    high = lax.ppermute(to_low, "space", [(i + 1, i) for i in range(count - 1)])
    fine, coarse = call(inner_kernel, [(13, 128, LANES), (8, 32, LANES)], [f32(5, 64, LANES)], u, *tables, cost=3000000)
    brick = (3, 128, LANES)
    new1, new2, payload, local = call(
        main_kernel, [brick, brick, (256, LANES), (12, 32, LANES)], [f32(6, 64, LANES)], u, *tables, fine, coarse, low, high, cost=3000000
    )
    slices = lax.axis_size("tm")
    behind = lax.ppermute(new2, "tm", [(i, i + 1) for i in range(slices - 1)])
    arrived = lax.all_to_all(payload, "tm", 0, 0, tiled=True)
    (starts,) = call(scan_kernel, [(128, LANES)], [f32(256, LANES), f32(3, 64, LANES)], arrived, local, cost=1000000)
    starts = lax.all_to_all(starts, "tm", 0, 0, tiled=True)
    outs, scratch = (9, 128, LANES), [f32(9, 128, LANES), f32(12, 64, LANES), pltpu.SemaphoreType.DMA((9,))]
    (out,) = call(finish_kernel, [outs], scratch, u, new1, new2, behind, local, starts, near_out=False, cost=1000000)
    return out.reshape(fine_nodes.shape)


def solution(mesh):
    whole = P("tm", None, None, "space", None, None)
    part = P("space", None, None)
    return jax.shard_map(
        on_device, mesh=mesh, in_specs=(whole, part, part, part), out_specs=whole, check_vma=False
    )
```

```python
import jax
import jax.numpy as jnp
from jax import lax
from jax.experimental import pallas as pl
from jax.experimental.pallas import tpu as pltpu
from jax.sharding import PartitionSpec as P

DT = 0.05
H = 0.5 * DT
KAPPA = ((1.0, 0.6, 1.4), (0.8, 1.2, 0.5), (0.7, 0.9, 1.1))
RATES = (0.5, 1.0, 0.3)
SIGNS = (-1.0, -0.5, 0.25)
Q1 = (DT * 5.0 / 24.0, DT / 3.0, -DT / 24.0)
Q2 = (-DT / 24.0, DT / 3.0, DT * 5.0 / 24.0)
Q3 = (DT / 6.0, DT * 2.0 / 3.0, DT / 6.0)
ROWS = 16
LANES = 128
EDGE = 18


def combine(weights, states):
    total = weights[0] * states[0]
    for w, s in zip(weights[1:], states[1:]):
        total = total + w * s
    return total


def shifted(v):
    rows = v.shape[0]
    y = lax.rem(lax.broadcasted_iota(jnp.int32, v.shape, 0), ROWS)
    z = lax.broadcasted_iota(jnp.int32, v.shape, 1)
    up = jnp.where(y == 0, 0.0, pltpu.roll(v, 1, 0))
    down = jnp.where(y == ROWS - 1, 0.0, pltpu.roll(v, rows - 1, 0))
    left = jnp.where(z == 0, 0.0, pltpu.roll(v, 1, 1))
    right = jnp.where(z == LANES - 1, 0.0, pltpu.roll(v, LANES - 1, 1))
    return (up + down) + (left + right)


def laplace(v):
    mid = v[ROWS:-ROWS]
    return v[: -2 * ROWS] + v[2 * ROWS :] + shifted(mid) - 6.0 * mid


def reaction(o, p, q):
    over = 0.5 * (p - 0.5 * q)
    return jnp.exp(over), jnp.exp(-over)


def current(state, film):
    fwd, bwd = reaction(*state)
    return film * state[0] * (fwd - bwd)


def conduct(region, k):
    return jnp.where(region == 0.0, KAPPA[k][0], jnp.where(region == 1.0, KAPPA[k][1], KAPPA[k][2]))


def inverse(mobile, k):
    return 1.0 - mobile * (H * RATES[k] / (1.0 + H * RATES[k]))


def first_new(old, lap, region, film, mobile):
    flow = combine(Q1, [current(old[m], film) for m in range(3)])
    news = []
    for k in range(3):
        w1 = combine(Q1, [old[m][k] for m in range(3)])
        inner = conduct(region, k) * lap[k] + SIGNS[k] * flow + RATES[k] * (H * old[1][k] - w1)
        news.append((old[0][k] + mobile * inner) * inverse(mobile, k))
    return news


def w2_of(old, k):
    return combine((Q2[0], Q2[1] - H, Q2[2]), [old[m][k] for m in range(3)])


def planes(lo, hi):
    return pl.ds(lo * ROWS, (hi - lo) * ROWS)


def copy_all(pairs, sems):
    copies = [pltpu.make_async_copy(src, dst, sems.at[i]) for i, (src, dst) in enumerate(pairs)]
    for copy in copies:
        copy.start()
    for copy in copies:
        copy.wait()


def edge_kernel(u_far, regions_far, activity_far, dirichlet_far, low_out, high_out, u, ints, activity, sems):
    pairs = []
    for side, three, two in ((0, 0, 0), (1, 5, 6)):
        wide, at = planes(three, three + 3), planes(two, two + 2)
        pairs.append((u_far.at[:, wide], u.at[side]))
        pairs.append((regions_far.at[at], ints.at[side, 0]))
        pairs.append((dirichlet_far.at[at], ints.at[side, 1]))
        pairs.append((activity_far.at[at], activity.at[side]))
    copy_all(pairs, sems)

    def tables(side, plane):
        at = planes(plane, plane + 1)
        region = ints[side, 0, at].astype(jnp.float32)
        film = jnp.where(region == 0.0, activity[side, at], 0.0)
        return region, film, 1.0 - ints[side, 1, at].astype(jnp.float32)

    mid = planes(1, 2)
    for side, out, edge in ((0, low_out, 0), (1, high_out, 2)):
        old = [[u[side, m * 3 + k, mid] for k in range(3)] for m in range(3)]
        lap = []
        for k in range(3):
            w1 = combine(Q1, [u[side, m * 3 + k] for m in range(3)])
            out[9 + k] = w1[ROWS : 2 * ROWS]
            lap.append(laplace(w1))
        news = first_new(old, lap, *tables(side, 1 - side))
        for k in range(3):
            out[12 + k] = H * news[k] + w2_of(old, k)
        end = planes(edge, edge + 1)
        for i in range(9):
            out[i] = u[side, i, end]
        for i, table in enumerate(tables(side, side)):
            out[15 + i] = table


def restrict(scratch, i, v):
    pairs = v.reshape(4, 2, ROWS, LANES)
    scratch[i] = (pairs[:, 0] + pairs[:, 1]).reshape(4 * ROWS, LANES)
    return 0.25 * (scratch[i, pl.ds(0, 32, stride=2)] + scratch[i, pl.ds(1, 32, stride=2)])


def inner_kernel(u, regions, activity, dirichlet, fine, coarse, scratch):
    region = regions[...].astype(jnp.float32)
    film = jnp.where(regions[...] == 0, activity[...], 0.0)
    mobile = 1.0 - dirichlet[...].astype(jnp.float32)
    old = [[u[m * 3 + k] for k in range(3)] for m in range(3)]
    zeros = jnp.zeros((ROWS, LANES), jnp.float32)
    lap1 = []
    for k in range(3):
        w1 = combine(Q1, [old[m][k] for m in range(3)])
        fine[9 + k] = w1
        lap1.append(laplace(jnp.concatenate([zeros, w1, zeros], axis=0)))
    new1 = first_new(old, lap1, region, film, mobile)
    flows = [current(old[m], film) for m in range(3)]
    flow2 = combine((Q2[0], Q2[1] - H, Q2[2]), flows)
    fine[12] = flows[0]
    for k in range(3):
        fine[k] = new1[k]
        fine[3 + k] = w2_of(old, k)
        decay = H * old[2][k] - combine(Q2, [old[m][k] for m in range(3)])
        fine[6 + k] = SIGNS[k] * flow2 + RATES[k] * decay
    zero = [restrict(scratch, k, old[0][k]) for k in range(3)]
    cfilm = restrict(scratch, 3, film)
    cmobile = restrict(scratch, 4, mobile)
    fwd, bwd = reaction(*zero)
    scale = (DT * cmobile) * cfilm
    coarse[0] = scale * (fwd - bwd)
    coarse[1] = scale * zero[0] * 0.5 * (fwd + bwd)
    coarse[2] = cmobile
    coarse[3] = cfilm
    coarse[4] = cfilm * zero[0] * (fwd - bwd)
    for k in range(3):
        coarse[5 + k] = zero[k]


def outer_new1(near, side):
    old = [[side[m * 3 + k] for k in range(3)] for m in range(3)]
    lap = []
    for k in range(3):
        w1 = combine(Q1, [old[m][k] for m in range(3)])
        lap.append(side[9 + k] + near[k] + shifted(w1) - 6.0 * w1)
    return first_new(old, lap, side[15], side[16], side[17])


def outer_rest(side):
    old = [[side[m * 3 + k] for k in range(3)] for m in range(3)]
    flow2 = combine((Q2[0], Q2[1] - H, Q2[2]), [current(old[m], side[16]) for m in range(3)])
    rest = []
    for k in range(3):
        decay = H * old[2][k] - combine(Q2, [old[m][k] for m in range(3)])
        rest.append(SIGNS[k] * flow2 + RATES[k] * decay)
    return rest, [w2_of(old, k) for k in range(3)]


def main_kernel(u, regions, activity, dirichlet, fine, coarse, low, high, new1_out, lower_out, upper_out, payload, local, scratch):
    def wrap(first, inside, last):
        return jnp.concatenate([first, inside, last], axis=0)

    own_region = regions[...].astype(jnp.float32)
    own_mobile = 1.0 - dirichlet[...].astype(jnp.float32)
    own_film = jnp.where(regions[...] == 0, activity[...], 0.0)
    region = wrap(low[15], own_region, high[15])
    film = wrap(low[16], own_film, high[16])
    mobile = wrap(low[17], own_mobile, high[17])
    first, last, between = slice(0, ROWS), slice(7 * ROWS, 8 * ROWS), slice(ROWS, 7 * ROWS)
    below = outer_new1([fine[9 + k, planes(0, 1)] for k in range(3)], low)
    above = outer_new1([fine[9 + k, planes(7, 8)] for k in range(3)], high)
    low_rest, low_w2 = outer_rest(low)
    high_rest, high_w2 = outer_rest(high)
    new1, own1 = [], []
    for k in range(3):
        v = fine[k]
        ends = []
        for at, side in ((first, low), (last, high)):
            factor = own_mobile[at] * inverse(own_mobile[at], k) * conduct(own_region[at], k)
            ends.append(v[at] + factor * combine(Q1, [side[m * 3 + k] for m in range(3)]))
        v = jnp.concatenate([ends[0], v[between], ends[1]], axis=0)
        own1.append(v)
        new1_out[k] = v
        new1.append(wrap(below[k], v, above[k]))
    flow1 = H * current(new1, film)
    new2, own2 = [], []
    for k in range(3):
        w2 = wrap(low_w2[k], fine[3 + k], high_w2[k])
        v2 = H * new1[k] + w2
        lap2 = laplace(jnp.concatenate([low[12 + k], v2, high[12 + k]], axis=0))
        rest = wrap(low_rest[k], fine[6 + k], high_rest[k])
        inner = conduct(region, k) * lap2 + SIGNS[k] * flow1 + rest
        v = (new1[k] + mobile * inner) * inverse(mobile, k)
        new2.append(v)
        own2.append(v[ROWS:-ROWS])
        lower_out[k] = own2[k][: 4 * ROWS]
        upper_out[k] = own2[k][4 * ROWS :]
    flow3 = Q3[0] * fine[12] + (Q3[1] / H) * flow1[ROWS:-ROWS] + Q3[2] * current(own2, own_film)
    integral, one = [], []
    for k in range(3):
        ends = [combine(Q3, [side[k], new1[k][at], new2[k][at]]) for side, at in ((low, slice(0, ROWS)), (high, slice(9 * ROWS, 10 * ROWS)))]
        v3 = combine(Q3, [u[k], own1[k], own2[k]])
        lap3 = laplace(wrap(ends[0], v3, ends[1]))
        force = own_mobile * (conduct(own_region, k) * lap3 + SIGNS[k] * flow3 - RATES[k] * v3)
        integral.append(restrict(scratch, k, force))
        one.append(restrict(scratch, 3 + k, own2[k]))
    a, b, cmobile, cfilm = (coarse[i] for i in range(4))
    zero = [coarse[5 + k] for k in range(3)]
    slope = a * zero[0] + b * (zero[1] - 0.5 * zero[2])
    flow_c = coarse[4] + current(one, cfilm)
    is_first = lax.axis_index("tm") == 0
    local[3] = a
    local[4] = b
    local[5] = cmobile
    sent = []
    for k in range(3):
        tend = H * cmobile * (SIGNS[k] * flow_c - RATES[k] * (zero[k] + one[k]))
        fas = integral[k] - tend
        term = (DT * RATES[k]) * cmobile * one[k] - SIGNS[k] * slope + tend + fas
        local[k] = term
        local[6 + k] = zero[k]
        local[9 + k] = one[k]
        sent.append(jnp.where(is_first, term + zero[k] + SIGNS[k] * slope, term))
    sent += [jnp.where(is_first, 0.0, a), jnp.where(is_first, 0.0, b), jnp.zeros_like(a)]
    lane = lax.broadcasted_iota(jnp.int32, (32, LANES), 1)
    half = lane < 64
    for m in range(3):
        x, y = sent[2 * m], sent[2 * m + 1]
        payload[pl.ds(m, 32, stride=6)] = jnp.where(half, x, pltpu.roll(y, 64, 1))
        payload[pl.ds(3 + m, 32, stride=6)] = jnp.where(half, pltpu.roll(x, 64, 1), y)


def scan_kernel(arrived, local, out, rolled, states):
    me = lax.axis_index("tm")
    row = local[5, pl.ds(me // 2, 1)]
    cmobile = jnp.where(lax.rem(me, 2) == 0, row, pltpu.roll(row, 64, 1))
    keep = [1.0 / (1.0 + (DT * RATES[k]) * cmobile) for k in range(3)]
    rolled[...] = pltpu.roll(arrived[...], 64, 1)
    v = [jnp.zeros((1, LANES), jnp.float32) for _ in range(3)]
    for n in range(64):
        for k in range(3):
            states[k, pl.ds(n, 1)] = v[k]
        term = [arrived[pl.ds(3 * n, 1)], rolled[pl.ds(3 * n, 1)], arrived[pl.ds(3 * n + 1, 1)]]
        a, b = rolled[pl.ds(3 * n + 1, 1)], arrived[pl.ds(3 * n + 2, 1)]
        t = a * v[0] + b * (v[1] - 0.5 * v[2])
        v = [keep[k] * (v[k] + term[k] + SIGNS[k] * t) for k in range(3)]
    half = lax.broadcasted_iota(jnp.int32, (64, LANES), 1) < 64
    out[pl.ds(0, 64, stride=2)] = jnp.where(half, states[0], pltpu.roll(states[1], 64, 1))
    out[pl.ds(1, 64, stride=2)] = states[2]


def finish_kernel(u, new1, lower, upper, lower_behind, upper_behind, local, starts, far, out, scratch, sems):
    is_first = lax.axis_index("tm") == 0
    half = lax.broadcasted_iota(jnp.int32, (32, LANES), 1) < 64
    rows = [starts[pl.ds(i, 32, stride=4)] for i in range(4)]
    start = [
        jnp.where(half, rows[0], pltpu.roll(rows[2], 64, 1)),
        jnp.where(half, pltpu.roll(rows[0], 64, 1), rows[2]),
        jnp.where(half, rows[1], pltpu.roll(rows[3], 64, 1)),
    ]
    start = [jnp.where(is_first, local[6 + k], start[k]) for k in range(3)]
    t = local[3] * start[0] + local[4] * (start[1] - 0.5 * start[2])

    def prolong(i, v):
        scratch[i, pl.ds(0, 32, stride=2)] = v
        scratch[i, pl.ds(1, 32, stride=2)] = v
        wide = scratch[i].reshape(4, 1, ROWS, LANES)
        return jnp.broadcast_to(wide, (4, 2, ROWS, LANES)).reshape(8 * ROWS, LANES)

    copies = []
    for k in range(3):
        end = (start[k] + local[k] + SIGNS[k] * t) / (1.0 + (DT * RATES[k]) * local[5])
        delta_zero = start[k] - local[6 + k]
        delta_one = end - local[9 + k]
        new2 = jnp.concatenate([lower[k], upper[k]], axis=0)
        head = jnp.where(is_first, u[k], jnp.concatenate([lower_behind[k], upper_behind[k]], axis=0))
        pairs = head.reshape(4, 2, ROWS, LANES)
        scratch[9 + k] = (pairs[:, 0] + pairs[:, 1]).reshape(4 * ROWS, LANES)
        coarse = 0.25 * (scratch[9 + k, pl.ds(0, 32, stride=2)] + scratch[9 + k, pl.ds(1, 32, stride=2)])
        parts = (
            head + prolong(3 * k, start[k] - coarse),
            new1[k] + prolong(3 * k + 1, 0.5 * (delta_zero + delta_one)),
            new2 + prolong(3 * k + 2, delta_one),
        )
        for m in range(3):
            out[3 * m + k] = parts[m]
            copy = pltpu.make_async_copy(out.at[3 * m + k], far.at[3 * m + k], sems.at[3 * m + k])
            copy.start()
            copies.append(copy)
    for copy in copies:
        copy.wait()


def call(kernel, outs, scratch, *args, near=True, near_out=True, cost=0, mib=32):
    vmem, hbm = pl.BlockSpec(memory_space=pltpu.VMEM), pl.BlockSpec(memory_space=pltpu.HBM)
    return pl.pallas_call(
        kernel,
        out_shape=[jax.ShapeDtypeStruct(s, jnp.float32) for s in outs],
        in_specs=[vmem if near else hbm] * len(args),
        out_specs=[vmem if near_out else hbm] * len(outs),
        scratch_shapes=scratch,
        compiler_params=pltpu.CompilerParams(vmem_limit_bytes=mib * 1024 * 1024),
        cost_estimate=pl.CostEstimate(flops=cost, bytes_accessed=cost, transcendentals=0),
    )(*args)


def f32(*shape):
    return pltpu.VMEM(shape, jnp.float32)


def on_device(fine_nodes, regions, activity, dirichlet):
    u = fine_nodes.reshape(9, 128, LANES)
    tables = [v.reshape(128, LANES) for v in (regions, activity, dirichlet)]
    edge = (EDGE, ROWS, LANES)
    buffers = [f32(2, 9, 48, LANES), pltpu.VMEM((2, 2, 32, LANES), jnp.int32), f32(2, 32, LANES), pltpu.SemaphoreType.DMA((8,))]
    pinned = [pltpu.with_memory_space_constraint(v, pltpu.HBM) for v in (u, *tables)]
    to_low, to_high = call(edge_kernel, [edge, edge], buffers, *pinned, near=False, cost=1000000, mib=32)
    count = lax.axis_size("space")
    low = lax.ppermute(to_high, "space", [(i, i + 1) for i in range(count - 1)])
    high = lax.ppermute(to_low, "space", [(i + 1, i) for i in range(count - 1)])
    fine, coarse = call(inner_kernel, [(13, 128, LANES), (8, 32, LANES)], [f32(5, 64, LANES)], u, *tables, cost=3000000)
    half = (3, 64, LANES)
    new1, lower, upper, payload, local = call(
        main_kernel, [(3, 128, LANES), half, half, (192, LANES), (12, 32, LANES)], [f32(6, 64, LANES)], u, *tables, fine, coarse, low, high, cost=3000000
    )
    nexts = [(i, i + 1) for i in range(lax.axis_size("tm") - 1)]
    lower_behind = lax.ppermute(lower, "tm", nexts)
    upper_behind = lax.ppermute(upper, "tm", nexts)
    arrived = lax.all_to_all(payload.reshape(64, 1, 3 * LANES), "tm", 0, 0, tiled=True).reshape(192, LANES)
    (starts,) = call(scan_kernel, [(128, LANES)], [f32(192, LANES), f32(3, 64, LANES)], arrived, local, cost=1000000)
    starts = lax.all_to_all(starts, "tm", 0, 0, tiled=True)
    outs, scratch = (9, 128, LANES), [f32(9, 128, LANES), f32(12, 64, LANES), pltpu.SemaphoreType.DMA((9,))]
    (out,) = call(finish_kernel, [outs], scratch, u, new1, lower, upper, lower_behind, upper_behind, local, starts, near_out=False, cost=1000000)
    return out.reshape(fine_nodes.shape)


def solution(mesh):
    whole = P("tm", None, None, "space", None, None)
    part = P("space", None, None)
    return jax.shard_map(
        on_device, mesh=mesh, in_specs=(whole, part, part, part), out_specs=whole, check_vma=False
    )
```

```python
import jax
import jax.numpy as jnp
from jax import lax
from jax.experimental import pallas as pl
from jax.experimental.pallas import tpu as pltpu
from jax.sharding import PartitionSpec as P

DT = 0.05
H = 0.5 * DT
KAPPA = ((1.0, 0.6, 1.4), (0.8, 1.2, 0.5), (0.7, 0.9, 1.1))
RATES = (0.5, 1.0, 0.3)
SIGNS = (-1.0, -0.5, 0.25)
Q1 = (DT * 5.0 / 24.0, DT / 3.0, -DT / 24.0)
Q2 = (-DT / 24.0, DT / 3.0, DT * 5.0 / 24.0)
Q3 = (DT / 6.0, DT * 2.0 / 3.0, DT / 6.0)
ROWS = 16
LANES = 128
EDGE = 15


def combine(weights, states):
    total = weights[0] * states[0]
    for w, s in zip(weights[1:], states[1:]):
        total = total + w * s
    return total


def shifted(v):
    rows = v.shape[0]
    y = lax.rem(lax.broadcasted_iota(jnp.int32, v.shape, 0), ROWS)
    z = lax.broadcasted_iota(jnp.int32, v.shape, 1)
    up = jnp.where(y == 0, 0.0, pltpu.roll(v, 1, 0))
    down = jnp.where(y == ROWS - 1, 0.0, pltpu.roll(v, rows - 1, 0))
    left = jnp.where(z == 0, 0.0, pltpu.roll(v, 1, 1))
    right = jnp.where(z == LANES - 1, 0.0, pltpu.roll(v, LANES - 1, 1))
    return (up + down) + (left + right)


def laplace(v):
    mid = v[ROWS:-ROWS]
    return v[: -2 * ROWS] + v[2 * ROWS :] + shifted(mid) - 6.0 * mid


def reaction(o, p, q):
    over = 0.5 * (p - 0.5 * q)
    return jnp.exp(over), jnp.exp(-over)


def current(state, film):
    fwd, bwd = reaction(*state)
    return film * state[0] * (fwd - bwd)


def conduct(region, k):
    return jnp.where(region == 0.0, KAPPA[k][0], jnp.where(region == 1.0, KAPPA[k][1], KAPPA[k][2]))


def inverse(mobile, k):
    return 1.0 - mobile * (H * RATES[k] / (1.0 + H * RATES[k]))


def first_new(old, lap, region, film, mobile):
    flow = combine(Q1, [current(old[m], film) for m in range(3)])
    news = []
    for k in range(3):
        w1 = combine(Q1, [old[m][k] for m in range(3)])
        inner = conduct(region, k) * lap[k] + SIGNS[k] * flow + RATES[k] * (H * old[1][k] - w1)
        news.append((old[0][k] + mobile * inner) * inverse(mobile, k))
    return news


def w2_of(old, k):
    return combine((Q2[0], Q2[1] - H, Q2[2]), [old[m][k] for m in range(3)])


def rest_of(old, flows):
    flow = combine((Q2[0], Q2[1] - H, Q2[2]), flows)
    rest = []
    for k in range(3):
        decay = H * old[2][k] - combine(Q2, [old[m][k] for m in range(3)])
        rest.append(SIGNS[k] * flow + RATES[k] * decay)
    return rest


def planes(lo, hi):
    return pl.ds(lo * ROWS, (hi - lo) * ROWS)


def copy_all(pairs, sems):
    copies = [pltpu.make_async_copy(src, dst, sems.at[i]) for i, (src, dst) in enumerate(pairs)]
    for copy in copies:
        copy.start()
    for copy in copies:
        copy.wait()


def edge_kernel(u_far, regions_far, activity_far, dirichlet_far, low_out, high_out, u, ints, activity, sems):
    pairs = []
    for side, three, two in ((0, 0, 0), (1, 5, 6)):
        wide, at = planes(three, three + 3), planes(two, two + 2)
        pairs.append((u_far.at[:, wide], u.at[side]))
        pairs.append((regions_far.at[at], ints.at[side, 0]))
        pairs.append((dirichlet_far.at[at], ints.at[side, 1]))
        pairs.append((activity_far.at[at], activity.at[side]))
    copy_all(pairs, sems)

    def tables(side, plane):
        at = planes(plane, plane + 1)
        region = ints[side, 0, at].astype(jnp.float32)
        film = jnp.where(region == 0.0, activity[side, at], 0.0)
        return region, film, 1.0 - ints[side, 1, at].astype(jnp.float32)

    mid = planes(1, 2)
    for side, out, edge in ((0, low_out, 0), (1, high_out, 2)):
        old = [[u[side, m * 3 + k, mid] for k in range(3)] for m in range(3)]
        w1 = [combine(Q1, [u[side, m * 3 + k] for m in range(3)]) for k in range(3)]
        news = first_new(old, [laplace(v) for v in w1], *tables(side, 1 - side))
        v2 = [H * news[k] + w2_of(old, k) for k in range(3)]
        end = planes(edge, edge + 1)
        old = [[u[side, m * 3 + k, end] for k in range(3)] for m in range(3)]
        region, film, mobile = tables(side, side)
        flows = [current(old[m], film) for m in range(3)]
        w1_end = [combine(Q1, [old[m][k] for m in range(3)]) for k in range(3)]
        lap = [w1[k][ROWS : 2 * ROWS] + shifted(w1_end[k]) - 6.0 * w1_end[k] for k in range(3)]
        partial = first_new(old, lap, region, film, mobile)
        rest = rest_of(old, flows)
        for k in range(3):
            w2 = w2_of(old, k)
            inner = conduct(region, k) * (v2[k] + shifted(w2) - 6.0 * w2) + rest[k]
            out[k] = w1_end[k]
            out[3 + k] = w2
            out[6 + k] = partial[k]
            out[9 + k] = old[0][k] + mobile * inner * inverse(mobile, k)
        out[12] = region
        out[13] = film
        out[14] = mobile


def restrict(scratch, i, v):
    pairs = v.reshape(4, 2, ROWS, LANES)
    scratch[i] = (pairs[:, 0] + pairs[:, 1]).reshape(4 * ROWS, LANES)
    return 0.25 * (scratch[i, pl.ds(0, 32, stride=2)] + scratch[i, pl.ds(1, 32, stride=2)])


def inner_kernel(u, regions, activity, dirichlet, fine, coarse, scratch):
    region = regions[...].astype(jnp.float32)
    film = jnp.where(regions[...] == 0, activity[...], 0.0)
    mobile = 1.0 - dirichlet[...].astype(jnp.float32)
    old = [[u[m * 3 + k] for k in range(3)] for m in range(3)]
    zeros = jnp.zeros((ROWS, LANES), jnp.float32)
    lap1 = []
    for k in range(3):
        w1 = combine(Q1, [old[m][k] for m in range(3)])
        fine[9 + k] = w1
        lap1.append(laplace(jnp.concatenate([zeros, w1, zeros], axis=0)))
    new1 = first_new(old, lap1, region, film, mobile)
    flows = [current(old[m], film) for m in range(3)]
    rest = rest_of(old, flows)
    fine[12] = flows[0]
    for k in range(3):
        fine[k] = new1[k]
        fine[3 + k] = w2_of(old, k)
        fine[6 + k] = rest[k]
    zero = [restrict(scratch, k, old[0][k]) for k in range(3)]
    cfilm = restrict(scratch, 3, film)
    cmobile = restrict(scratch, 4, mobile)
    fwd, bwd = reaction(*zero)
    scale = (DT * cmobile) * cfilm
    coarse[0] = scale * (fwd - bwd)
    coarse[1] = scale * zero[0] * 0.5 * (fwd + bwd)
    coarse[2] = cmobile
    coarse[3] = cfilm
    coarse[4] = cfilm * zero[0] * (fwd - bwd)
    for k in range(3):
        coarse[5 + k] = zero[k]


def outer_plane(side, w1):
    region, film, mobile = side[12], side[13], side[14]
    gain = [mobile * inverse(mobile, k) for k in range(3)]
    flow = [gain[k] * conduct(region, k) for k in range(3)]
    new1 = [side[6 + k] + flow[k] * w1[k] for k in range(3)]
    v2 = [H * new1[k] + side[3 + k] for k in range(3)]
    return new1, v2, flow, gain, H * current(new1, film), mobile


def outer_v3(side, outer, v2):
    new1, _, flow, gain, cur, mobile = outer
    v3 = []
    for k in range(3):
        spread = v2[k] + H * (shifted(new1[k]) - 6.0 * new1[k])
        total = side[9 + k] + new1[k] * inverse(mobile, k) + flow[k] * spread + gain[k] * (SIGNS[k] * cur)
        v3.append(Q3[0] * total + Q3[1] * new1[k])
    return v3


def main_kernel(u, regions, activity, dirichlet, fine, coarse, low, high, new1_out, lower_out, upper_out, payload, local, scratch):
    region = regions[...].astype(jnp.float32)
    mobile = 1.0 - dirichlet[...].astype(jnp.float32)
    film = jnp.where(regions[...] == 0, activity[...], 0.0)
    first, last, between = slice(0, ROWS), slice(7 * ROWS, 8 * ROWS), slice(ROWS, 7 * ROWS)
    below = outer_plane(low, [fine[9 + k, planes(0, 1)] for k in range(3)])
    above = outer_plane(high, [fine[9 + k, planes(7, 8)] for k in range(3)])
    new1, v2 = [], []
    for k in range(3):
        v = fine[k]
        ends = []
        for at, side in ((first, low), (last, high)):
            factor = mobile[at] * inverse(mobile[at], k) * conduct(region[at], k)
            ends.append(v[at] + factor * side[k])
        v = jnp.concatenate([ends[0], v[between], ends[1]], axis=0)
        new1.append(v)
        new1_out[k] = v
        v2.append(H * v + fine[3 + k])
    flow1 = H * current(new1, film)
    new2 = []
    for k in range(3):
        lap2 = laplace(jnp.concatenate([below[1][k], v2[k], above[1][k]], axis=0))
        inner = conduct(region, k) * lap2 + SIGNS[k] * flow1 + fine[6 + k]
        v = (new1[k] + mobile * inner) * inverse(mobile, k)
        new2.append(v)
        lower_out[k] = v[: 4 * ROWS]
        upper_out[k] = v[4 * ROWS :]
    flow3 = Q3[0] * fine[12] + (Q3[1] / H) * flow1 + Q3[2] * current(new2, film)
    v3_low = outer_v3(low, below, [v[first] for v in v2])
    v3_high = outer_v3(high, above, [v[last] for v in v2])
    integral, one = [], []
    for k in range(3):
        v3 = combine(Q3, [u[k], new1[k], new2[k]])
        lap3 = laplace(jnp.concatenate([v3_low[k], v3, v3_high[k]], axis=0))
        force = mobile * (conduct(region, k) * lap3 + SIGNS[k] * flow3 - RATES[k] * v3)
        integral.append(restrict(scratch, k, force))
        one.append(restrict(scratch, 3 + k, new2[k]))
    a, b, cmobile, cfilm = (coarse[i] for i in range(4))
    zero = [coarse[5 + k] for k in range(3)]
    slope = a * zero[0] + b * (zero[1] - 0.5 * zero[2])
    flow_c = coarse[4] + current(one, cfilm)
    is_first = lax.axis_index("tm") == 0
    local[3] = a
    local[4] = b
    local[5] = cmobile
    sent = []
    for k in range(3):
        tend = H * cmobile * (SIGNS[k] * flow_c - RATES[k] * (zero[k] + one[k]))
        fas = integral[k] - tend
        term = (DT * RATES[k]) * cmobile * one[k] - SIGNS[k] * slope + tend + fas
        local[k] = term
        local[6 + k] = zero[k]
        local[9 + k] = one[k]
        sent.append(jnp.where(is_first, term + zero[k] + SIGNS[k] * slope, term))
    sent += [jnp.where(is_first, 0.0, a), jnp.where(is_first, 0.0, b), jnp.zeros_like(a)]
    lane = lax.broadcasted_iota(jnp.int32, (32, LANES), 1)
    half = lane < 64
    for m in range(3):
        x, y = sent[2 * m], sent[2 * m + 1]
        payload[pl.ds(m, 32, stride=6)] = jnp.where(half, x, pltpu.roll(y, 64, 1))
        payload[pl.ds(3 + m, 32, stride=6)] = jnp.where(half, pltpu.roll(x, 64, 1), y)


def scan_kernel(arrived, local, out, rolled, states, segments):
    me = lax.axis_index("tm")
    row = local[5, pl.ds(me // 2, 1)]
    cmobile = jnp.where(lax.rem(me, 2) == 0, row, pltpu.roll(row, 64, 1))
    keep = [1.0 / (1.0 + (DT * RATES[k]) * cmobile) for k in range(3)]
    push = [keep[k] * SIGNS[k] for k in range(3)]
    rolled[...] = pltpu.roll(arrived[...], 64, 1)

    def rows(ref, t, m):
        return ref[pl.ds(3 * t + m, 8, stride=24)]

    terms = [[rows(arrived, t, 0), rows(rolled, t, 0), rows(arrived, t, 1)] for t in range(8)]
    terms = [[keep[k] * term[k] for k in range(3)] for term in terms]
    slopes = [(rows(rolled, t, 1), rows(arrived, t, 2)) for t in range(8)]

    def advance(t, v):
        a, b = slopes[t]
        slope = a * v[0] + b * (v[1] - 0.5 * v[2])
        return [keep[k] * v[k] + push[k] * slope for k in range(3)]

    a, b = slopes[0]
    columns = [[push[k] * f for k in range(3)] for f in (a, b, -0.5 * b)]
    for k in range(3):
        columns[k][k] = columns[k][k] + keep[k]
    part = terms[0]
    for t in range(1, 8):
        columns = [advance(t, column) for column in columns]
        part = [x + y for x, y in zip(advance(t, part), terms[t])]
    for k in range(3):
        for m, column in enumerate((*columns, part)):
            segments[4 * k + m] = column[k]
    v = [segments[4 * k + 3, 0:1] for k in range(3)]
    for k in range(3):
        segments[12 + k, 0:1] = jnp.zeros_like(v[k])
    for g in range(1, 8):
        at = slice(g, g + 1)
        for k in range(3):
            segments[12 + k, at] = v[k]
        if g < 7:
            moved = []
            for k in range(3):
                left = segments[4 * k, at] * v[0] + segments[4 * k + 1, at] * v[1]
                moved.append(left + (segments[4 * k + 2, at] * v[2] + segments[4 * k + 3, at]))
            v = moved
    v = [segments[12 + k] for k in range(3)]
    for t in range(8):
        for k in range(3):
            states[k, pl.ds(t, 8, stride=8)] = v[k]
        if t < 7:
            v = [x + y for x, y in zip(advance(t, v), terms[t])]
    half = lax.broadcasted_iota(jnp.int32, (64, LANES), 1) < 64
    out[pl.ds(0, 64, stride=2)] = jnp.where(half, states[0], pltpu.roll(states[1], 64, 1))
    out[pl.ds(1, 64, stride=2)] = states[2]


def prolong(scratch, i, v):
    scratch[i, pl.ds(0, 32, stride=2)] = v
    scratch[i, pl.ds(1, 32, stride=2)] = v
    wide = scratch[i].reshape(4, 1, ROWS, LANES)
    return jnp.broadcast_to(wide, (4, 2, ROWS, LANES)).reshape(8 * ROWS, LANES)


def base_kernel(u, new1, lower, upper, lower_behind, upper_behind, local, out, scratch):
    is_first = lax.axis_index("tm") == 0
    for k in range(3):
        new2 = jnp.concatenate([lower[k], upper[k]], axis=0)
        head = jnp.where(is_first, u[k], jnp.concatenate([lower_behind[k], upper_behind[k]], axis=0))
        zero, one = local[6 + k], local[9 + k]
        out[k] = head - prolong(scratch, 3 * k, restrict(scratch, 9 + k, head))
        out[3 + k] = new1[k] - prolong(scratch, 3 * k + 1, 0.5 * (zero + one))
        out[6 + k] = new2 - prolong(scratch, 3 * k + 2, one)


def finish_kernel(base, local, starts, far, out, scratch, sems):
    is_first = lax.axis_index("tm") == 0
    half = lax.broadcasted_iota(jnp.int32, (32, LANES), 1) < 64
    rows = [starts[pl.ds(i, 32, stride=4)] for i in range(4)]
    start = [
        jnp.where(half, rows[0], pltpu.roll(rows[2], 64, 1)),
        jnp.where(half, pltpu.roll(rows[0], 64, 1), rows[2]),
        jnp.where(half, rows[1], pltpu.roll(rows[3], 64, 1)),
    ]
    start = [jnp.where(is_first, local[6 + k], start[k]) for k in range(3)]
    t = local[3] * start[0] + local[4] * (start[1] - 0.5 * start[2])
    copies = []
    for k in range(3):
        end = (start[k] + local[k] + SIGNS[k] * t) / (1.0 + (DT * RATES[k]) * local[5])
        for m, v in enumerate((start[k], 0.5 * (start[k] + end), end)):
            i = 3 * m + k
            out[i] = base[i] + prolong(scratch, i, v)
            copy = pltpu.make_async_copy(out.at[i], far.at[i], sems.at[i])
            copy.start()
            copies.append(copy)
    for copy in copies:
        copy.wait()


def call(kernel, outs, scratch, *args, near=True, near_out=True, cost=0, mib=32):
    vmem, hbm = pl.BlockSpec(memory_space=pltpu.VMEM), pl.BlockSpec(memory_space=pltpu.HBM)
    return pl.pallas_call(
        kernel,
        out_shape=[jax.ShapeDtypeStruct(s, jnp.float32) for s in outs],
        in_specs=[vmem if near else hbm] * len(args),
        out_specs=[vmem if near_out else hbm] * len(outs),
        scratch_shapes=scratch,
        compiler_params=pltpu.CompilerParams(vmem_limit_bytes=mib * 1024 * 1024),
        cost_estimate=pl.CostEstimate(flops=cost, bytes_accessed=cost, transcendentals=0),
    )(*args)


def f32(*shape):
    return pltpu.VMEM(shape, jnp.float32)


def on_device(fine_nodes, regions, activity, dirichlet):
    u = fine_nodes.reshape(9, 128, LANES)
    tables = [v.reshape(128, LANES) for v in (regions, activity, dirichlet)]
    edge = (EDGE, ROWS, LANES)
    buffers = [f32(2, 9, 48, LANES), pltpu.VMEM((2, 2, 32, LANES), jnp.int32), f32(2, 32, LANES), pltpu.SemaphoreType.DMA((8,))]
    pinned = [pltpu.with_memory_space_constraint(v, pltpu.HBM) for v in (u, *tables)]
    to_low, to_high = call(edge_kernel, [edge, edge], buffers, *pinned, near=False, cost=1000000, mib=32)
    count = lax.axis_size("space")
    low = lax.ppermute(to_high, "space", [(i, i + 1) for i in range(count - 1)])
    high = lax.ppermute(to_low, "space", [(i + 1, i) for i in range(count - 1)])
    fine, coarse = call(inner_kernel, [(13, 128, LANES), (8, 32, LANES)], [f32(5, 64, LANES)], u, *tables, cost=3000000)
    half = (3, 64, LANES)
    new1, lower, upper, payload, local = call(
        main_kernel, [(3, 128, LANES), half, half, (192, LANES), (12, 32, LANES)], [f32(6, 64, LANES)], u, *tables, fine, coarse, low, high, cost=3000000
    )
    nexts = [(i, i + 1) for i in range(lax.axis_size("tm") - 1)]
    lower_behind = lax.ppermute(lower, "tm", nexts)
    upper_behind = lax.ppermute(upper, "tm", nexts)
    arrived = lax.all_to_all(payload.reshape(64, 1, 3 * LANES), "tm", 0, 0, tiled=True).reshape(192, LANES)
    scratch = [f32(192, LANES), f32(3, 64, LANES), f32(15, 8, LANES)]
    (starts,) = call(scan_kernel, [(128, LANES)], scratch, arrived, local, cost=1000000)
    whole, scratch = (9, 128, LANES), f32(12, 64, LANES)
    fine_parts = (u, new1, lower, upper, lower_behind, upper_behind)
    (base,) = call(base_kernel, [whole], [scratch], *fine_parts, local, cost=1000000)
    starts = lax.all_to_all(starts, "tm", 0, 0, tiled=True)
    scratch = [f32(*whole), scratch, pltpu.SemaphoreType.DMA((9,))]
    (out,) = call(finish_kernel, [whole], scratch, base, local, starts, near_out=False, cost=1000000)
    return out.reshape(fine_nodes.shape)


def solution(mesh):
    whole = P("tm", None, None, "space", None, None)
    part = P("space", None, None)
    return jax.shard_map(
        on_device, mesh=mesh, in_specs=(whole, part, part, part), out_specs=whole, check_vma=False
    )
```

```python
import jax
import jax.numpy as jnp
from jax import lax
from jax.experimental import pallas as pl
from jax.experimental.pallas import tpu as pltpu
from jax.sharding import PartitionSpec as P

DT = 0.05
H = 0.5 * DT
KAPPA = ((1.0, 0.6, 1.4), (0.8, 1.2, 0.5), (0.7, 0.9, 1.1))
RATES = (0.5, 1.0, 0.3)
SIGNS = (-1.0, -0.5, 0.25)
Q1 = (DT * 5.0 / 24.0, DT / 3.0, -DT / 24.0)
Q2 = (-DT / 24.0, DT / 3.0, DT * 5.0 / 24.0)
Q3 = (DT / 6.0, DT * 2.0 / 3.0, DT / 6.0)
ROWS = 16
LANES = 128
EDGE = 15


def combine(weights, states):
    total = weights[0] * states[0]
    for w, s in zip(weights[1:], states[1:]):
        total = total + w * s
    return total


def shifted(v):
    rows = v.shape[0]
    y = lax.rem(lax.broadcasted_iota(jnp.int32, v.shape, 0), ROWS)
    z = lax.broadcasted_iota(jnp.int32, v.shape, 1)
    up = jnp.where(y == 0, 0.0, pltpu.roll(v, 1, 0))
    down = jnp.where(y == ROWS - 1, 0.0, pltpu.roll(v, rows - 1, 0))
    left = jnp.where(z == 0, 0.0, pltpu.roll(v, 1, 1))
    right = jnp.where(z == LANES - 1, 0.0, pltpu.roll(v, LANES - 1, 1))
    return (up + down) + (left + right)


def laplace(v):
    mid = v[ROWS:-ROWS]
    return v[: -2 * ROWS] + v[2 * ROWS :] + shifted(mid) - 6.0 * mid


def reaction(o, p, q):
    over = 0.5 * (p - 0.5 * q)
    return jnp.exp(over), jnp.exp(-over)


def current(state, film):
    fwd, bwd = reaction(*state)
    return film * state[0] * (fwd - bwd)


def conduct(region, k):
    return jnp.where(region == 0.0, KAPPA[k][0], jnp.where(region == 1.0, KAPPA[k][1], KAPPA[k][2]))


def inverse(mobile, k):
    return 1.0 - mobile * (H * RATES[k] / (1.0 + H * RATES[k]))


def first_new(old, lap, region, film, mobile):
    flow = combine(Q1, [current(old[m], film) for m in range(3)])
    news = []
    for k in range(3):
        w1 = combine(Q1, [old[m][k] for m in range(3)])
        inner = conduct(region, k) * lap[k] + SIGNS[k] * flow + RATES[k] * (H * old[1][k] - w1)
        news.append((old[0][k] + mobile * inner) * inverse(mobile, k))
    return news


def w2_of(old, k):
    return combine((Q2[0], Q2[1] - H, Q2[2]), [old[m][k] for m in range(3)])


def rest_of(old, flows):
    flow = combine((Q2[0], Q2[1] - H, Q2[2]), flows)
    rest = []
    for k in range(3):
        decay = H * old[2][k] - combine(Q2, [old[m][k] for m in range(3)])
        rest.append(SIGNS[k] * flow + RATES[k] * decay)
    return rest


def planes(lo, hi):
    return pl.ds(lo * ROWS, (hi - lo) * ROWS)


def copy_all(pairs, sems):
    copies = [pltpu.make_async_copy(src, dst, sems.at[i]) for i, (src, dst) in enumerate(pairs)]
    for copy in copies:
        copy.start()
    for copy in copies:
        copy.wait()


def edge_kernel(u_far, regions_far, activity_far, dirichlet_far, low_out, high_out, u, ints, activity, sems):
    pairs = []
    for side, three, two in ((0, 0, 0), (1, 5, 6)):
        wide, at = planes(three, three + 3), planes(two, two + 2)
        pairs.append((u_far.at[:, wide], u.at[side]))
        pairs.append((regions_far.at[at], ints.at[side, 0]))
        pairs.append((dirichlet_far.at[at], ints.at[side, 1]))
        pairs.append((activity_far.at[at], activity.at[side]))
    copy_all(pairs, sems)

    def tables(side, plane):
        at = planes(plane, plane + 1)
        region = ints[side, 0, at].astype(jnp.float32)
        film = jnp.where(region == 0.0, activity[side, at], 0.0)
        return region, film, 1.0 - ints[side, 1, at].astype(jnp.float32)

    mid = planes(1, 2)
    for side, out, edge in ((0, low_out, 0), (1, high_out, 2)):
        old = [[u[side, m * 3 + k, mid] for k in range(3)] for m in range(3)]
        w1 = [combine(Q1, [u[side, m * 3 + k] for m in range(3)]) for k in range(3)]
        news = first_new(old, [laplace(v) for v in w1], *tables(side, 1 - side))
        v2 = [H * news[k] + w2_of(old, k) for k in range(3)]
        end = planes(edge, edge + 1)
        old = [[u[side, m * 3 + k, end] for k in range(3)] for m in range(3)]
        region, film, mobile = tables(side, side)
        flows = [current(old[m], film) for m in range(3)]
        w1_end = [combine(Q1, [old[m][k] for m in range(3)]) for k in range(3)]
        lap = [w1[k][ROWS : 2 * ROWS] + shifted(w1_end[k]) - 6.0 * w1_end[k] for k in range(3)]
        partial = first_new(old, lap, region, film, mobile)
        rest = rest_of(old, flows)
        for k in range(3):
            w2 = w2_of(old, k)
            inner = conduct(region, k) * (v2[k] + shifted(w2) - 6.0 * w2) + rest[k]
            out[k] = w1_end[k]
            out[3 + k] = w2
            out[6 + k] = partial[k]
            out[9 + k] = old[0][k] + mobile * inner * inverse(mobile, k)
        out[12] = region
        out[13] = film
        out[14] = mobile


def restrict(scratch, i, v):
    pairs = v.reshape(4, 2, ROWS, LANES)
    scratch[i] = (pairs[:, 0] + pairs[:, 1]).reshape(4 * ROWS, LANES)
    return 0.25 * (scratch[i, pl.ds(0, 32, stride=2)] + scratch[i, pl.ds(1, 32, stride=2)])


def inner_kernel(u_far, regions_far, activity_far, dirichlet_far, fine, coarse, scratch, u, ints, acts, sems):
    copy_all([(u_far, u), (regions_far, ints.at[0]), (dirichlet_far, ints.at[1]), (activity_far, acts)], sems)
    region = ints[0].astype(jnp.float32)
    film = jnp.where(region == 0.0, acts[...], 0.0)
    mobile = 1.0 - ints[1].astype(jnp.float32)
    fine[13] = region
    fine[14] = film
    fine[15] = mobile
    old = [[u[m * 3 + k] for k in range(3)] for m in range(3)]
    zeros = jnp.zeros((ROWS, LANES), jnp.float32)
    lap1 = []
    for k in range(3):
        w1 = combine(Q1, [old[m][k] for m in range(3)])
        fine[9 + k] = w1
        lap1.append(laplace(jnp.concatenate([zeros, w1, zeros], axis=0)))
    new1 = first_new(old, lap1, region, film, mobile)
    flows = [current(old[m], film) for m in range(3)]
    rest = rest_of(old, flows)
    fine[12] = flows[0]
    for k in range(3):
        fine[k] = new1[k]
        fine[16 + k] = old[0][k]
        fine[3 + k] = w2_of(old, k)
        fine[6 + k] = rest[k]
    zero = [restrict(scratch, k, old[0][k]) for k in range(3)]
    cfilm = restrict(scratch, 3, film)
    cmobile = restrict(scratch, 4, mobile)
    fwd, bwd = reaction(*zero)
    scale = (DT * cmobile) * cfilm
    coarse[0] = scale * (fwd - bwd)
    coarse[1] = scale * zero[0] * 0.5 * (fwd + bwd)
    coarse[2] = cmobile
    coarse[3] = cfilm
    coarse[4] = cfilm * zero[0] * (fwd - bwd)
    for k in range(3):
        coarse[5 + k] = zero[k]


def outer_plane(side, w1):
    region, film, mobile = side[12], side[13], side[14]
    gain = [mobile * inverse(mobile, k) for k in range(3)]
    flow = [gain[k] * conduct(region, k) for k in range(3)]
    new1 = [side[6 + k] + flow[k] * w1[k] for k in range(3)]
    v2 = [H * new1[k] + side[3 + k] for k in range(3)]
    return new1, v2, flow, gain, H * current(new1, film), mobile


def outer_v3(side, outer, v2):
    new1, _, flow, gain, cur, mobile = outer
    v3 = []
    for k in range(3):
        spread = v2[k] + H * (shifted(new1[k]) - 6.0 * new1[k])
        total = side[9 + k] + new1[k] * inverse(mobile, k) + flow[k] * spread + gain[k] * (SIGNS[k] * cur)
        v3.append(Q3[0] * total + Q3[1] * new1[k])
    return v3


def main_kernel(fine, coarse, low, high, new1_out, lower_out, upper_out, payload, local, scratch):
    region, film, mobile = fine[13], fine[14], fine[15]
    first, last, between = slice(0, ROWS), slice(7 * ROWS, 8 * ROWS), slice(ROWS, 7 * ROWS)
    below = outer_plane(low, [fine[9 + k, planes(0, 1)] for k in range(3)])
    above = outer_plane(high, [fine[9 + k, planes(7, 8)] for k in range(3)])
    new1, v2 = [], []
    for k in range(3):
        v = fine[k]
        ends = []
        for at, side in ((first, low), (last, high)):
            factor = mobile[at] * inverse(mobile[at], k) * conduct(region[at], k)
            ends.append(v[at] + factor * side[k])
        v = jnp.concatenate([ends[0], v[between], ends[1]], axis=0)
        new1.append(v)
        new1_out[k] = v
        v2.append(H * v + fine[3 + k])
    flow1 = H * current(new1, film)
    new2 = []
    for k in range(3):
        lap2 = laplace(jnp.concatenate([below[1][k], v2[k], above[1][k]], axis=0))
        inner = conduct(region, k) * lap2 + SIGNS[k] * flow1 + fine[6 + k]
        v = (new1[k] + mobile * inner) * inverse(mobile, k)
        new2.append(v)
        lower_out[k] = v[: 4 * ROWS]
        upper_out[k] = v[4 * ROWS :]
    flow3 = Q3[0] * fine[12] + (Q3[1] / H) * flow1 + Q3[2] * current(new2, film)
    v3_low = outer_v3(low, below, [v[first] for v in v2])
    v3_high = outer_v3(high, above, [v[last] for v in v2])
    integral, one = [], []
    for k in range(3):
        v3 = combine(Q3, [fine[16 + k], new1[k], new2[k]])
        lap3 = laplace(jnp.concatenate([v3_low[k], v3, v3_high[k]], axis=0))
        force = mobile * (conduct(region, k) * lap3 + SIGNS[k] * flow3 - RATES[k] * v3)
        integral.append(restrict(scratch, k, force))
        one.append(restrict(scratch, 3 + k, new2[k]))
    a, b, cmobile, cfilm = (coarse[i] for i in range(4))
    zero = [coarse[5 + k] for k in range(3)]
    slope = a * zero[0] + b * (zero[1] - 0.5 * zero[2])
    flow_c = coarse[4] + current(one, cfilm)
    is_first = lax.axis_index("tm") == 0
    local[3] = a
    local[4] = b
    local[5] = cmobile
    sent = []
    for k in range(3):
        tend = H * cmobile * (SIGNS[k] * flow_c - RATES[k] * (zero[k] + one[k]))
        fas = integral[k] - tend
        term = (DT * RATES[k]) * cmobile * one[k] - SIGNS[k] * slope + tend + fas
        local[k] = term
        local[6 + k] = zero[k]
        local[9 + k] = one[k]
        sent.append(jnp.where(is_first, term + zero[k] + SIGNS[k] * slope, term))
    sent += [jnp.where(is_first, 0.0, a), jnp.where(is_first, 0.0, b), jnp.zeros_like(a)]
    lane = lax.broadcasted_iota(jnp.int32, (32, LANES), 1)
    half = lane < 64
    for m in range(3):
        x, y = sent[2 * m], sent[2 * m + 1]
        payload[pl.ds(m, 32, stride=6)] = jnp.where(half, x, pltpu.roll(y, 64, 1))
        payload[pl.ds(3 + m, 32, stride=6)] = jnp.where(half, pltpu.roll(x, 64, 1), y)


def scan_kernel(arrived, local, out, rolled, states, segments):
    me = lax.axis_index("tm")
    row = local[5, pl.ds(me // 2, 1)]
    cmobile = jnp.where(lax.rem(me, 2) == 0, row, pltpu.roll(row, 64, 1))
    keep = [1.0 / (1.0 + (DT * RATES[k]) * cmobile) for k in range(3)]
    push = [keep[k] * SIGNS[k] for k in range(3)]
    rolled[...] = pltpu.roll(arrived[...], 64, 1)

    def rows(ref, t, m):
        return ref[pl.ds(3 * t + m, 8, stride=24)]

    terms = [[rows(arrived, t, 0), rows(rolled, t, 0), rows(arrived, t, 1)] for t in range(8)]
    terms = [[keep[k] * term[k] for k in range(3)] for term in terms]
    slopes = [(rows(rolled, t, 1), rows(arrived, t, 2)) for t in range(8)]

    def advance(t, v):
        a, b = slopes[t]
        slope = a * v[0] + b * (v[1] - 0.5 * v[2])
        return [keep[k] * v[k] + push[k] * slope for k in range(3)]

    a, b = slopes[0]
    columns = [[push[k] * f for k in range(3)] for f in (a, b, -0.5 * b)]
    for k in range(3):
        columns[k][k] = columns[k][k] + keep[k]
    part = terms[0]
    for t in range(1, 8):
        columns = [advance(t, column) for column in columns]
        part = [x + y for x, y in zip(advance(t, part), terms[t])]
    for k in range(3):
        for m, column in enumerate((*columns, part)):
            segments[4 * k + m] = column[k]
    v = [segments[4 * k + 3, 0:1] for k in range(3)]
    for k in range(3):
        segments[12 + k, 0:1] = jnp.zeros_like(v[k])
    for g in range(1, 8):
        at = slice(g, g + 1)
        for k in range(3):
            segments[12 + k, at] = v[k]
        if g < 7:
            moved = []
            for k in range(3):
                left = segments[4 * k, at] * v[0] + segments[4 * k + 1, at] * v[1]
                moved.append(left + (segments[4 * k + 2, at] * v[2] + segments[4 * k + 3, at]))
            v = moved
    v = [segments[12 + k] for k in range(3)]
    for t in range(8):
        for k in range(3):
            states[k, pl.ds(t, 8, stride=8)] = v[k]
        if t < 7:
            v = [x + y for x, y in zip(advance(t, v), terms[t])]
    half = lax.broadcasted_iota(jnp.int32, (64, LANES), 1) < 64
    out[pl.ds(0, 64, stride=2)] = jnp.where(half, states[0], pltpu.roll(states[1], 64, 1))
    out[pl.ds(1, 64, stride=2)] = states[2]


def prolong(scratch, i, v):
    scratch[i, pl.ds(0, 32, stride=2)] = v
    scratch[i, pl.ds(1, 32, stride=2)] = v
    wide = scratch[i].reshape(4, 1, ROWS, LANES)
    return jnp.broadcast_to(wide, (4, 2, ROWS, LANES)).reshape(8 * ROWS, LANES)


def base_kernel(fine, new1, lower, upper, lower_behind, upper_behind, local, out, scratch):
    is_first = lax.axis_index("tm") == 0
    for k in range(3):
        new2 = jnp.concatenate([lower[k], upper[k]], axis=0)
        head = jnp.where(is_first, fine[16 + k], jnp.concatenate([lower_behind[k], upper_behind[k]], axis=0))
        zero, one = local[6 + k], local[9 + k]
        out[k] = head - prolong(scratch, 3 * k, restrict(scratch, 9 + k, head))
        out[3 + k] = new1[k] - prolong(scratch, 3 * k + 1, 0.5 * (zero + one))
        out[6 + k] = new2 - prolong(scratch, 3 * k + 2, one)


def finish_kernel(base, local, starts, far, out, scratch, sems):
    is_first = lax.axis_index("tm") == 0
    half = lax.broadcasted_iota(jnp.int32, (32, LANES), 1) < 64
    rows = [starts[pl.ds(i, 32, stride=4)] for i in range(4)]
    start = [
        jnp.where(half, rows[0], pltpu.roll(rows[2], 64, 1)),
        jnp.where(half, pltpu.roll(rows[0], 64, 1), rows[2]),
        jnp.where(half, rows[1], pltpu.roll(rows[3], 64, 1)),
    ]
    start = [jnp.where(is_first, local[6 + k], start[k]) for k in range(3)]
    t = local[3] * start[0] + local[4] * (start[1] - 0.5 * start[2])
    copies = []
    for k in range(3):
        end = (start[k] + local[k] + SIGNS[k] * t) / (1.0 + (DT * RATES[k]) * local[5])
        for m, v in enumerate((start[k], 0.5 * (start[k] + end), end)):
            i = 3 * m + k
            out[i] = base[i] + prolong(scratch, i, v)
            copy = pltpu.make_async_copy(out.at[i], far.at[i], sems.at[i])
            copy.start()
            copies.append(copy)
    for copy in copies:
        copy.wait()


def call(kernel, outs, scratch, *args, near=True, near_out=True, cost=0, mib=32):
    vmem, hbm = pl.BlockSpec(memory_space=pltpu.VMEM), pl.BlockSpec(memory_space=pltpu.HBM)
    return pl.pallas_call(
        kernel,
        out_shape=[jax.ShapeDtypeStruct(s, jnp.float32) for s in outs],
        in_specs=[vmem if near else hbm] * len(args),
        out_specs=[vmem if near_out else hbm] * len(outs),
        scratch_shapes=scratch,
        compiler_params=pltpu.CompilerParams(vmem_limit_bytes=mib * 1024 * 1024),
        cost_estimate=pl.CostEstimate(flops=cost, bytes_accessed=cost, transcendentals=0),
    )(*args)


def f32(*shape):
    return pltpu.VMEM(shape, jnp.float32)


def on_device(fine_nodes, regions, activity, dirichlet):
    u = fine_nodes.reshape(9, 128, LANES)
    tables = [v.reshape(128, LANES) for v in (regions, activity, dirichlet)]
    edge = (EDGE, ROWS, LANES)
    buffers = [f32(2, 9, 48, LANES), pltpu.VMEM((2, 2, 32, LANES), jnp.int32), f32(2, 32, LANES), pltpu.SemaphoreType.DMA((8,))]
    pinned = [pltpu.with_memory_space_constraint(v, pltpu.HBM) for v in (u, *tables)]
    to_low, to_high = call(edge_kernel, [edge, edge], buffers, *pinned, near=False, cost=1000000, mib=32)
    count = lax.axis_size("space")
    low = lax.ppermute(to_high, "space", [(i, i + 1) for i in range(count - 1)])
    high = lax.ppermute(to_low, "space", [(i + 1, i) for i in range(count - 1)])
    buffers = [f32(5, 64, LANES), f32(9, 128, LANES), pltpu.VMEM((2, 128, LANES), jnp.int32), f32(128, LANES), pltpu.SemaphoreType.DMA((4,))]
    fine, coarse = call(inner_kernel, [(19, 128, LANES), (8, 32, LANES)], buffers, *pinned, near=False, cost=3000000)
    half = (3, 64, LANES)
    new1, lower, upper, payload, local = call(
        main_kernel, [(3, 128, LANES), half, half, (192, LANES), (12, 32, LANES)], [f32(6, 64, LANES)], fine, coarse, low, high, cost=3000000
    )
    nexts = [(i, i + 1) for i in range(lax.axis_size("tm") - 1)]
    lower_behind = lax.ppermute(lower, "tm", nexts)
    upper_behind = lax.ppermute(upper, "tm", nexts)
    arrived = lax.all_to_all(payload.reshape(64, 1, 3 * LANES), "tm", 0, 0, tiled=True).reshape(192, LANES)
    scratch = [f32(192, LANES), f32(3, 64, LANES), f32(15, 8, LANES)]
    (starts,) = call(scan_kernel, [(128, LANES)], scratch, arrived, local, cost=1000000)
    whole, scratch = (9, 128, LANES), f32(12, 64, LANES)
    fine_parts = (fine, new1, lower, upper, lower_behind, upper_behind)
    (base,) = call(base_kernel, [whole], [scratch], *fine_parts, local, cost=1000000)
    starts = lax.all_to_all(starts, "tm", 0, 0, tiled=True)
    scratch = [f32(*whole), scratch, pltpu.SemaphoreType.DMA((9,))]
    (out,) = call(finish_kernel, [whole], scratch, base, local, starts, near_out=False, cost=1000000)
    return out.reshape(fine_nodes.shape)


def solution(mesh):
    whole = P("tm", None, None, "space", None, None)
    part = P("space", None, None)
    return jax.shard_map(
        on_device, mesh=mesh, in_specs=(whole, part, part, part), out_specs=whole, check_vma=False
    )
```
